256 devices in a mesh: blk: 32 (over y_lo, z, core), dp: 8 (over y_hi, x).
Axes of the slice: x: 4, y: 4 (y_hi: 2, y_lo: 2; y = y_hi * 2 + y_lo), z: 8, core: 2. Of those that a mesh axis runs over, the one named last changes fastest.
Arguments:
- queries: bfloat16 [8, 4096, 512], P('dp', 'blk'), may hold values from -10 to 10
- prefix_keys: bfloat16 [4096, 128], P('blk'), may hold values from -8 to 8
- prefix_values: bfloat16 [4096, 128], P('blk'), may hold values from -6 to 6
- hidden: bfloat16 [8, 4096, 8192], P('dp', None, 'blk'), may hold values from -6 to 6
- out_grad: bfloat16 [8, 4096, 8192], P('dp', None, 'blk'), may hold values from -6 to 6
- prefix_hidden: bfloat16 [4096, 8192], P('blk', 'dp'), may hold values from -0.059814453 to 0.059814453
- w_query: bfloat16 [8192, 512], P('blk'), may hold values from -0.75 to 0.75
- w_out: bfloat16 [512, 8192], P(None, 'blk'), may hold values from -0.0625 to 0.0625
Outputs:
- grad_hidden: bfloat16 [8, 4096, 8192], P('dp', None, 'blk')
- grad_wq: float32 [8192, 512], P(('blk', 'dp'))
- grad_wo: float32 [512, 8192], P('dp', 'blk')
- grad_prefix_kv: bfloat16 [4096, 256], P('blk')
- grad_wkv: float32 [256, 8192], P('blk', 'dp')
The draws below stay inside these ranges and needn't reach their ends.
All inputs are finite; a program needn't handle non-finite values.
Results may differ from the reference program's by a relative error of at most 0.03.
Values may be sent and summed in bfloat16 or wider, within the bound.
No kernel may reach another device: no remote copies, remote signals or barrier semaphores. Data moves between devices by JAX's collectives and lax.ppermute only.
A program may use at most 128 MiB of HBM per device.

```python
import math
import jax
import jax.numpy as jnp
from jax import lax

D = 8192
H = 4
HD = 128
HQ = 512
CH = 4096
SPANS = 8
PREFIX = 4096


def draw_queries(key, part):
    key = jax.random.fold_in(key, 5)
    row_scale = jnp.exp(jax.random.uniform(jax.random.fold_in(key, 1), (SPANS, CH, 1), jnp.float32, math.log(0.5), math.log(2.0)))
    drawn = jnp.clip(jax.random.normal(jax.random.fold_in(key, 2), (SPANS, CH, HQ), jnp.float32), -5.0, 5.0) * row_scale
    return drawn.astype(jnp.bfloat16)


def draw_prefix_keys(key, part):
    key = jax.random.fold_in(key, 9)
    ramp = 1.0 + 2.0 * jnp.arange(PREFIX, dtype=jnp.float32)[:, None] / PREFIX
    row_scale = ramp * jnp.exp(jax.random.uniform(jax.random.fold_in(key, 1), (PREFIX, 1), jnp.float32, math.log(0.25), math.log(1.25)))
    drawn = jnp.clip(jax.random.normal(jax.random.fold_in(key, 2), (PREFIX, HD), jnp.float32), -2.1, 2.1) * row_scale
    return drawn.astype(jnp.bfloat16)


def strengthened(entries, rng, source, target, blocks, factor):
    owner, partner = [(jnp.arange(entries.shape[dim]) // (entries.shape[dim] // blocks)).reshape([-1 if axis == dim else 1 for axis in range(entries.ndim)]) for dim in (source, target)]
    chosen = jax.random.permutation(rng, blocks)[partner]
    strong = (owner == chosen) | (owner == (partner + blocks // 2) % blocks)
    return jnp.where(strong, factor * entries, entries)


def block_scale(stream_key, dims, cuts, low, high):
    level, own = 1.0, jax.random.fold_in(stream_key, 6)
    for dim, shards_of in cuts:
        heights = jnp.exp(jax.random.uniform(jax.random.fold_in(own, dim), (shards_of,), jnp.float32, low / len(cuts), high / len(cuts)))
        level = level * jnp.repeat(heights, dims[dim] // shards_of).reshape([-1 if axis == dim else 1 for axis in range(len(dims))])
    return level


def normal_values(rng, shape, deviation, limit, shards=(), held_as=jnp.bfloat16):
    result = jax.random.normal(rng, shape, jnp.float32) * deviation
    if len(shards) > 0:
        result = block_scale(rng, shape, shards, -0.22, 0.18) * result
    return jnp.clip(result, min=-limit, max=limit).astype(held_as)


def gaussian_with(stream_key, shape, scale, limit, shards, heavy, kind=jnp.bfloat16):
    result = scale * jax.random.normal(stream_key, shape, jnp.float32)
    if shards:
        result = result * block_scale(stream_key, shape, shards, -0.22, 0.18)
    return jnp.clip(strengthened(result, jax.random.fold_in(stream_key, 3), *heavy), -limit, limit).astype(kind)


def setup_inputs(seed: int = 0) -> dict:
    key_list = jax.random.split(jax.random.key(seed), 9)
    queries = draw_queries(jax.random.fold_in(key_list[8], 71), 0)
    prefix_keys = draw_prefix_keys(jax.random.fold_in(key_list[8], 71), 0)
    prefix_values = normal_values(key_list[2], (PREFIX, HD), 1.0, 6.0, ((0, 32),))
    hidden = normal_values(key_list[3], (SPANS, CH, D), 1.0, 6.0, ((0, 8), (2, 32)))
    out_grad = gaussian_with(key_list[4], (SPANS, CH, D), 1.0, 6.0, ((0, 8), (2, 32)), (2, 1, 32, 2.75))
    prefix_hidden = normal_values(key_list[5], (PREFIX, D), 0.01, 0.059814453, ((0, 32), (1, 8)))
    w_query = normal_values(key_list[6], (D, HQ), 0.125, 0.75, ((0, 32),))
    w_out = normal_values(key_list[7], (HQ, D), D ** -0.5, 0.0625, ((1, 32),))
    return dict(queries=queries, prefix_keys=prefix_keys, prefix_values=prefix_values, hidden=hidden, out_grad=out_grad, prefix_hidden=prefix_hidden, w_query=w_query, w_out=w_out)


def rounded(value):
    return lax.optimization_barrier(value.astype(jnp.bfloat16)).astype(jnp.float32)


def to_rows(split_value):
    return split_value.transpose(1, 0, 2).reshape(CH, HQ)


def span_grads(query_rows, grad_rows, prefix_keys, prefix_values):
    scale_factor = HD ** -0.5
    heads_q = query_rows.astype(jnp.float32).reshape(CH, H, HD).transpose(1, 0, 2)
    key_rows = prefix_keys.astype(jnp.float32)
    value_rows = prefix_values.astype(jnp.float32)
    scores = jnp.einsum('hid,jd->hij', heads_q, key_rows) * scale_factor
    row_max = jnp.max(scores, axis=-1, keepdims=True)
    log_total = row_max + jnp.log(jnp.sum(jnp.exp(scores - row_max), axis=-1, keepdims=True))
    soft_weights = jnp.exp(scores - log_total)
    probs_low = rounded(soft_weights)
    outputs = jnp.einsum('hij,jd->hid', probs_low, value_rows).astype(jnp.bfloat16)
    grad_out = grad_rows.astype(jnp.float32).reshape(CH, H, HD).transpose(1, 0, 2)
    row_delta = jnp.sum(grad_out * outputs.astype(jnp.float32), axis=-1, keepdims=True)
    grad_probs = jnp.einsum('hid,jd->hij', grad_out, value_rows)
    grad_scores = rounded(soft_weights * (grad_probs - row_delta) * scale_factor)
    grad_values = jnp.einsum('hij,hid->jd', probs_low, grad_out)
    grad_keys = jnp.einsum('hij,hid->jd', grad_scores, heads_q)
    grad_queries = jnp.einsum('hij,jd->hid', grad_scores, key_rows).astype(jnp.bfloat16)
    return to_rows(outputs), to_rows(grad_queries), jnp.concatenate([grad_keys, grad_values], axis=1)


def reference(queries, prefix_keys, prefix_values, hidden, out_grad, prefix_hidden, w_query, w_out):
    def per_span(carried, pieces):
        grad_wq, grad_wo, grad_kv = carried
        query_rows, hidden_rows, upstream = pieces
        grad_rows = jnp.dot(upstream, w_out.T, preferred_element_type=jnp.float32).astype(jnp.bfloat16)
        outputs, grad_queries, kv_part = span_grads(query_rows, grad_rows, prefix_keys, prefix_values)
        grad_input = jnp.dot(grad_queries, w_query.T, preferred_element_type=jnp.float32).astype(jnp.bfloat16)
        grad_wq = grad_wq + jnp.dot(hidden_rows.T, grad_queries, preferred_element_type=jnp.float32)
        grad_wo = grad_wo + jnp.dot(outputs.T, upstream, preferred_element_type=jnp.float32)
        return (grad_wq, grad_wo, grad_kv + kv_part), grad_input

    initial = (jnp.zeros((D, HQ), jnp.float32), jnp.zeros((HQ, D), jnp.float32),
               jnp.zeros((PREFIX, 2 * HD), jnp.float32))
    (grad_wq, grad_wo, grad_kv), grad_hidden = lax.scan(per_span, initial, (queries, hidden, out_grad))
    grad_prefix_kv = grad_kv.astype(jnp.bfloat16)
    grad_wkv = jnp.dot(grad_prefix_kv.T, prefix_hidden, preferred_element_type=jnp.float32)
    return grad_hidden, grad_wq, grad_wo, grad_prefix_kv, grad_wkv
```

```python
import math

import jax
import jax.numpy as jnp
from jax import lax
from jax.experimental import pallas as pl
from jax.experimental.pallas import tpu as pltpu
from jax.sharding import PartitionSpec as P

BF = jnp.bfloat16
F32 = jnp.float32
NZ = 8
HEADS = 4
HD = 128
RB = 128
SCALE = HD ** -0.5
SCALE2 = SCALE * math.log2(math.e)
KEY_CHUNK = 512
PARAMS = pltpu.CompilerParams(vmem_limit_bytes=56 * 1024 * 1024)

NN = (((1,), (0,)), ((), ()))
NT = (((1,), (1,)), ((), ()))
TN = (((0,), (0,)), ((), ()))


def dot(a, b, dims):
    return lax.dot_general(a, b, dims, preferred_element_type=F32)


def blk_perm(move):
    pairs = []
    for i in range(32):
        y, z, c = move(i // 16, (i // 2) % 8, i % 2)
        pairs.append((i, (y * 8 + z % 8) * 2 + c))
    return pairs


UP = blk_perm(lambda y, z, c: (y, z + 1, c))
DOWN = blk_perm(lambda y, z, c: (y, z - 1, c))
ACROSS = blk_perm(lambda y, z, c: (1 - y, z, c))
SIBLING = blk_perm(lambda y, z, c: (y, z, 1 - c))
DP_X1 = [(i, i ^ 1) for i in range(8)]
DP_X2 = [(i, i ^ 2) for i in range(8)]
DP_Y = [(i, i ^ 4) for i in range(8)]


def send(value, pairs):
    return lax.ppermute(value, "blk", pairs)


def added(*terms):
    total = terms[0].astype(F32)
    for term in terms[1:]:
        total = total + term.astype(F32)
    return total.astype(BF)


def z_gather(block):
    half = block.shape[0] // 2
    up1, down1 = send(block, UP), send(block, DOWN)
    up2, down2 = send(up1, UP), send(down1, DOWN)
    up3, down3 = send(up2, UP), send(down2, DOWN)
    up4, down4 = send(up3[:half], UP), send(down3[half:], DOWN)
    return [block, down1, down2, down3, (up4, down4), up3, up2, up1]


def z_scatter(parts):
    half = parts[0].shape[0] // 2
    up, down = send(parts[4][:half], UP), send(parts[4][half:], DOWN)
    up = jnp.concatenate([added(parts[3][:half], up), parts[3][half:]], axis=0)
    down = jnp.concatenate([parts[5][:half], added(parts[5][half:], down)], axis=0)
    up, down = send(up, UP), send(down, DOWN)
    up, down = send(added(parts[2], up), UP), send(added(parts[6], down), DOWN)
    up, down = send(added(parts[1], up), UP), send(added(parts[7], down), DOWN)
    return parts[0], up, down


def whole(count):
    return [pl.BlockSpec(memory_space=pltpu.VMEM)] * count


def call(kernel, place, operands, outs, scratch=(), flops=0, moved=0, exps=0):
    return pl.pallas_call(
        kernel,
        in_specs=[pl.BlockSpec(memory_space=pltpu.SMEM)] + whole(len(operands)),
        out_specs=tuple(whole(len(outs))),
        out_shape=tuple(outs),
        scratch_shapes=list(scratch),
        compiler_params=PARAMS,
        cost_estimate=pl.CostEstimate(flops=flops, bytes_accessed=moved, transcendentals=exps),
    )(place, *operands)


def upstream_kernel(place, og, og_sib, w_own, w_sib, part, og_cat):
    z, c = place[1], place[2]
    width = og.shape[1]
    for y in range(2):
        for k in range(NZ):
            slot = y * NZ + lax.rem(z + k, NZ)
            rows = pl.ds((y * NZ + k) * RB, RB)
            og_cat[rows, :width] = og[pl.ds(pl.multiple_of((slot * 2 + c) * RB, RB), RB), :]
            og_cat[rows, width:] = og_sib[pl.ds(pl.multiple_of(slot * RB, RB), RB), :]
    step = 512
    for i in range(2 * NZ * RB // step):
        rows = pl.ds(i * step, step)
        got = dot(og_cat[rows, :width], w_own[...], NT) + dot(og_cat[rows, width:], w_sib[...], NT)
        part[rows, :] = got.astype(BF)


def stacked(rows):
    return jnp.concatenate([rows[:, h * HD:(h + 1) * HD] for h in range(HEADS)], axis=0)


def forward_kernel(place, q, kv_own, kv_sib, out, log_total, scores):
    qs = stacked(q[...])
    lanes = HEADS * RB
    top = jnp.full((1, lanes), -jnp.inf, F32)
    count = kv_own.shape[0] // KEY_CHUNK
    chunks = [(ref, i) for ref in (kv_own, kv_sib) for i in range(count)]
    for n, (ref, i) in enumerate(chunks):
        got = dot(ref[pl.ds(i * KEY_CHUNK, KEY_CHUNK), :HD], qs, NT)
        scores[pl.ds(n * KEY_CHUNK, KEY_CHUNK), :] = got
        top = jnp.maximum(top, jnp.max(got, axis=0, keepdims=True))
    total = jnp.zeros((1, lanes), F32)
    acc = jnp.zeros((HD, lanes), F32)
    for n, (ref, i) in enumerate(chunks):
        weights = jnp.exp2((scores[pl.ds(n * KEY_CHUNK, KEY_CHUNK), :] - top) * SCALE2)
        total = total + jnp.sum(weights, axis=0, keepdims=True)
        acc = acc + dot(ref[pl.ds(i * KEY_CHUNK, KEY_CHUNK), HD:], weights.astype(BF), TN)
    acc = acc / total
    for h in range(HEADS):
        out[:, h * HD:(h + 1) * HD] = acc[:, h * RB:(h + 1) * RB].T.astype(BF)
    log_total[...] = top * SCALE2 + jnp.log2(total)


def backward_kernel(place, q, kv_own, kv_sib, g, o, log_total, dq, dkv_own, dkv_sib):
    qs = stacked(q[...])
    gs = stacked(g[...])
    lanes = HEADS * RB
    products = g[...].astype(F32) * o[...].astype(F32)
    delta = jnp.concatenate(
        [jnp.sum(products[:, h * HD:(h + 1) * HD].T, axis=0, keepdims=True) for h in range(HEADS)],
        axis=1,
    )
    shift = log_total[...]
    acc = jnp.zeros((HD, lanes), F32)
    count = kv_own.shape[0] // KEY_CHUNK
    for ref, dref in ((kv_own, dkv_own), (kv_sib, dkv_sib)):
        for i in range(count):
            rows = pl.ds(i * KEY_CHUNK, KEY_CHUNK)
            keys, values = ref[rows, :HD], ref[rows, HD:]
            probs = jnp.exp2(dot(keys, qs, NT) * SCALE2 - shift)
            dref[rows, HD:] = dot(probs.astype(BF), gs, NN).astype(BF)
            ds = (probs * (dot(values, gs, NT) - delta)).astype(BF)
            dref[rows, :HD] = (dot(ds, qs, NN) * SCALE).astype(BF)
            acc = acc + dot(keys, ds, TN)
    acc = acc * SCALE
    for h in range(HEADS):
        dq[:, h * HD:(h + 1) * HD] = acc[:, h * RB:(h + 1) * RB].T.astype(BF)


def wo_kernel(place, o_own, o_far, og_cat, part_own, part_sib):
    y = place[0]
    size = o_own.shape[0]
    width = part_own.shape[1]
    near = og_cat[pl.ds(pl.multiple_of(y * size, size), size), :]
    far = og_cat[pl.ds(pl.multiple_of((1 - y) * size, size), size), :]
    got = dot(o_own[...], near, TN) + dot(o_far[...], far, TN)
    part_own[...] = got[:, :width].astype(BF)
    part_sib[...] = got[:, width:].astype(BF)


def hidden_kernel(place, hidden, w, *refs):
    grad_hidden, part = refs[-3], refs[-2]
    acc = refs[-1]
    blocks = refs[:-3]
    z, c = place[1], place[2]
    acc[...] = jnp.zeros_like(acc)
    for side in range(2):
        owner = c if side == 0 else 1 - c
        for k in range(NZ):
            if k < 4:
                rows = blocks[side * 9 + k][...]
            elif k == 4:
                rows = jnp.concatenate([blocks[side * 9 + 4][...], blocks[side * 9 + 5][...]], axis=0)
            else:
                rows = blocks[side * 9 + k + 1][...]
            slot = lax.rem(z + k, NZ)
            low = pl.ds(pl.multiple_of((slot * 2 + owner) * RB, RB), RB)
            high = pl.ds(pl.multiple_of(((NZ + slot) * 2 + owner) * RB, RB), RB)
            got = dot(rows, w[...], NT).astype(BF)
            grad_hidden[low, :] = got[:RB]
            grad_hidden[high, :] = got[RB:]
            inputs = jnp.concatenate([hidden[low, :], hidden[high, :]], axis=0)
            acc[...] += dot(inputs, rows, TN)
    part[...] = acc[...].astype(BF)


def dp_scatter(part):
    rows, columns = part.shape
    got = lax.all_to_all(part.reshape(8, rows // 8, columns), "dp", 0, 0)
    return jnp.sum(got.astype(F32), axis=0)


def shards(queries, prefix_keys, prefix_values, hidden, out_grad, prefix_hidden, w_query, w_out):
    me = lax.axis_index("blk")
    y, z, c = me // 16, (me // 2) % 8, me % 2
    place = jnp.stack([y, z, c]).astype(jnp.int32)
    q = queries[0]
    og = out_grad[0]
    rows, width = og.shape
    hq = q.shape[1]
    half = rows // 2
    bf = lambda *shape: jax.ShapeDtypeStruct(shape, BF)

    kv = jnp.concatenate([prefix_keys, prefix_values], axis=1)
    kv_far = send(kv, ACROSS)
    kv_pair = jnp.where(y == 0, jnp.concatenate([kv, kv_far]), jnp.concatenate([kv_far, kv]))

    given = lax.dynamic_index_in_dim(og.reshape(16, 2, RB, width), 1 - c, 1, keepdims=False)
    og_sib = send(given.reshape(half, width), SIBLING)
    w_sib = send(w_out, SIBLING)

    kv_blocks = z_gather(kv_pair)
    kv_blocks[4] = jnp.concatenate(kv_blocks[4])
    kv_own = jnp.concatenate(kv_blocks)
    kv_sib = send(kv_own, SIBLING)

    g_part, og_cat = call(
        upstream_kernel, place, (og, og_sib, w_out, w_sib), (bf(half, hq), bf(half, 2 * width)),
        flops=2 * half * hq * 2 * width, moved=8 << 20,
    )
    g_part = g_part.reshape(2, NZ, RB, hq)
    g_own, g_up, g_down = z_scatter([g_part[:, k].reshape(2 * RB, hq) for k in range(NZ)])
    g_sum = added(g_own, g_up, g_down).reshape(2, RB, hq)
    g_far = send(lax.dynamic_index_in_dim(g_sum, 1 - y, 0, keepdims=False), ACROSS)
    g = added(lax.dynamic_index_in_dim(g_sum, y, 0, keepdims=False), g_far)

    o, log_total = call(
        forward_kernel, place, (q, kv_own, kv_sib),
        (bf(RB, hq), jax.ShapeDtypeStruct((1, HEADS * RB), F32)),
        scratch=[pltpu.VMEM((rows, HEADS * RB), F32)],
        flops=4 * HEADS * RB * rows * HD, moved=3 << 20, exps=HEADS * RB * rows,
    )
    o_blocks = z_gather(o)
    o_blocks[4] = jnp.concatenate(o_blocks[4])
    o_own = jnp.concatenate(o_blocks)
    o_far = send(o_own, ACROSS)

    dq, dkv_own, dkv_sib = call(
        backward_kernel, place, (q, kv_own, kv_sib, g, o, log_total),
        (bf(RB, hq), bf(half, 2 * HD), bf(half, 2 * HD)),
        flops=10 * HEADS * RB * rows * HD, moved=6 << 20, exps=HEADS * RB * rows,
    )

    dq_far = send(dq, ACROSS)
    dq_pair = jnp.where(y == 0, jnp.concatenate([dq, dq_far]), jnp.concatenate([dq_far, dq]))

    dkv_got = send(dkv_sib, SIBLING)
    dkv_sum = added(dkv_own, dkv_got).reshape(NZ, 2 * RB, 2 * HD)
    dkv_mine, dkv_up, dkv_down = z_scatter([dkv_sum[k] for k in range(NZ)])
    dkv = added(dkv_mine, dkv_up, dkv_down).reshape(2, RB, 2 * HD)
    dkv_far = send(lax.dynamic_index_in_dim(dkv, 1 - y, 0, keepdims=False), ACROSS)
    dkv = lax.dynamic_index_in_dim(dkv, y, 0, keepdims=False).astype(F32) + dkv_far.astype(F32)
    for pairs in (DP_X1, DP_X2, DP_Y):
        dkv = dkv + lax.ppermute(dkv, "dp", pairs)
    kv_low = dkv.astype(BF)

    dq_blocks = z_gather(dq_pair)
    flat = dq_blocks[:4] + list(dq_blocks[4]) + dq_blocks[5:]
    other = [send(block, SIBLING) for block in flat]
    grad_hidden, wq_part = call(
        hidden_kernel, place, (hidden[0], w_query, *flat, *other),
        (bf(rows, width), bf(width, hq)),
        scratch=[pltpu.VMEM((width, hq), F32)],
        flops=4 * rows * width * hq, moved=8 << 20,
    )

    wo_own, wo_sib = call(
        wo_kernel, place, (o_own, o_far, og_cat), (bf(hq, width), bf(hq, width)),
        flops=2 * half * hq * 2 * width, moved=5 << 20,
    )
    wo_part = added(wo_own, send(wo_sib, SIBLING))
    grad_wo = dp_scatter(wo_part)
    grad_wq = dp_scatter(wq_part)

    kv_cols = kv_low.T.reshape(2, NZ, 2, 8, RB)
    kv_cols = jnp.roll(kv_cols, -z, axis=1)
    columns = prefix_hidden.shape[1]
    wkv = dot(kv_cols.reshape(2 * HD, RB), prefix_hidden, NN).astype(BF).reshape(2, NZ, 2, 8, columns)
    wkv_got = send(lax.dynamic_index_in_dim(wkv, 1 - c, 2, keepdims=False), SIBLING)
    wkv = added(lax.dynamic_index_in_dim(wkv, c, 2, keepdims=False), wkv_got)
    wkv_far = send(lax.dynamic_index_in_dim(wkv, 1 - y, 0, keepdims=False), ACROSS)
    wkv = added(lax.dynamic_index_in_dim(wkv, y, 0, keepdims=False), wkv_far)
    wkv = wkv.reshape(NZ, 16, columns // 2)
    wkv_mine, wkv_up, wkv_down = z_scatter([wkv[k] for k in range(NZ)])
    grad_wkv = wkv_mine.astype(F32) + wkv_up.astype(F32) + wkv_down.astype(F32)
    return grad_hidden[None], grad_wq, grad_wo, kv_low, grad_wkv.reshape(8, columns)


def solution(mesh):
    in_specs = (
        P("dp", "blk", None),
        P("blk", None),
        P("blk", None),
        P("dp", None, "blk"),
        P("dp", None, "blk"),
        P("blk", "dp"),
        P("blk", None),
        P(None, "blk"),
    )
    out_specs = (
        P("dp", None, "blk"),
        P(("blk", "dp"), None),
        P("dp", "blk"),
        P("blk", None),
        P("blk", "dp"),
    )
    return jax.shard_map(shards, mesh=mesh, in_specs=in_specs, out_specs=out_specs, check_vma=False)
```

```python
import functools
import math

import jax
import jax.numpy as jnp
from jax import lax
from jax.experimental import pallas as pl
from jax.experimental.pallas import tpu as pltpu
from jax.sharding import PartitionSpec as P

BF = jnp.bfloat16
F32 = jnp.float32
NZ = 8
HEADS = 4
HD = 128
RB = 128
SCALE = HD ** -0.5
SCALE2 = SCALE * math.log2(math.e)
KEY_CHUNK = 512
PARAMS = pltpu.CompilerParams(vmem_limit_bytes=56 * 1024 * 1024)

NN = (((1,), (0,)), ((), ()))
NT = (((1,), (1,)), ((), ()))
TN = (((0,), (0,)), ((), ()))


def dot(a, b, dims):
    return lax.dot_general(a, b, dims, preferred_element_type=F32)


def blk_perm(move):
    pairs = []
    for i in range(32):
        y, z, c = move(i // 16, (i // 2) % 8, i % 2)
        pairs.append((i, (y * 8 + z % 8) * 2 + c))
    return pairs


UP = blk_perm(lambda y, z, c: (y, z + 1, c))
DOWN = blk_perm(lambda y, z, c: (y, z - 1, c))
ACROSS = blk_perm(lambda y, z, c: (1 - y, z, c))
SIBLING = blk_perm(lambda y, z, c: (y, z, 1 - c))
DP_X1 = [(i, i ^ 1) for i in range(8)]
DP_X2 = [(i, i ^ 2) for i in range(8)]
DP_Y = [(i, i ^ 4) for i in range(8)]


def send(value, pairs):
    return lax.ppermute(value, "blk", pairs)


def added(*terms):
    total = terms[0].astype(F32)
    for term in terms[1:]:
        total = total + term.astype(F32)
    return total.astype(BF)


def z_gather(block):
    half = block.shape[0] // 2
    up1, down1 = send(block, UP), send(block, DOWN)
    up2, down2 = send(up1, UP), send(down1, DOWN)
    up3, down3 = send(up2, UP), send(down2, DOWN)
    up4, down4 = send(up3[:half], UP), send(down3[half:], DOWN)
    return [block, down1, down2, down3, (up4, down4), up3, up2, up1]


def whole(count):
    return [pl.BlockSpec(memory_space=pltpu.VMEM)] * count


def call(kernel, place, operands, outs, scratch=(), flops=0, moved=0, exps=0, unread=0):
    return pl.pallas_call(
        kernel,
        in_specs=[pl.BlockSpec(memory_space=pltpu.SMEM)] + whole(len(operands) - unread)
        + [pl.BlockSpec(memory_space=pl.ANY)] * unread,
        out_specs=tuple(whole(len(outs))),
        out_shape=tuple(outs),
        scratch_shapes=list(scratch),
        compiler_params=PARAMS,
        cost_estimate=pl.CostEstimate(flops=flops, bytes_accessed=moved, transcendentals=exps),
    )(place, *operands)


def bf(*shape):
    return jax.ShapeDtypeStruct(shape, BF)


def f32(*shape):
    return jax.ShapeDtypeStruct(shape, F32)


def upstream_kernel(offsets, place, og, og_sib, w_own, w_sib, *refs):
    outs = refs[-len(offsets):]
    z, c = place[1], place[2]
    for k, out in zip(offsets, outs):
        own, far = [], []
        for y in range(2):
            slot = y * NZ + lax.rem(z + k, NZ)
            own.append(og[pl.ds(pl.multiple_of((slot * 2 + c) * RB, RB), RB), :])
            far.append(og_sib[pl.ds(pl.multiple_of(slot * RB, RB), RB), :])
        own, far = jnp.concatenate(own, axis=0), jnp.concatenate(far, axis=0)
        out[...] = (dot(own, w_own[...], NT) + dot(far, w_sib[...], NT)).astype(BF)


def plus(a, b):
    return (a.astype(F32) + b.astype(F32)).astype(BF)


def step_a_kernel(place, part, kv_up, kv_down, up, down):
    up[:RB, :] = part[:RB, :]
    up[RB:, :] = kv_up[...]
    down[:RB, :] = part[RB:, :]
    down[RB:, :] = kv_down[...]


def step_b_kernel(place, got_up, got_down, part_up, part_down, up, down):
    up[:RB, :] = plus(part_up[:RB, :], got_up[:RB, :])
    up[RB:2 * RB, :] = part_up[RB:, :]
    up[2 * RB:, :] = got_up[RB:RB + 32, :]
    down[:RB, :] = part_down[:RB, :]
    down[RB:2 * RB, :] = plus(part_down[RB:, :], got_down[:RB, :])
    down[2 * RB:, :] = got_down[RB + 32:, :]


def step_c_kernel(place, got_up, got_down, part_up, part_down, up, down):
    up[...] = plus(part_up[...], got_up[:2 * RB, :])
    down[...] = plus(part_down[...], got_down[:2 * RB, :])


def kv_kernel(place, own, up1, up2, down1, down2, a_up, a_down, b_up, b_down, out):
    out[0:64, :] = own[...]
    out[64:128, :] = down1[...]
    out[128:192, :] = down2[...]
    out[192:256, :] = a_down[RB:, :]
    out[256:288, :] = b_up[2 * RB:, :]
    out[288:320, :] = b_down[2 * RB:, :]
    out[320:384, :] = a_up[RB:, :]
    out[384:448, :] = up2[...]
    out[448:512, :] = up1[...]


def owned_kernel(place, part, got_up, got_down, near, far):
    y = place[0]
    for side, out in ((y, near), (1 - y, far)):
        rows = pl.ds(pl.multiple_of(side * RB, RB), RB)
        total = part[rows, :].astype(F32) + got_up[rows, :].astype(F32) + got_down[rows, :].astype(F32)
        out[...] = total.astype(BF)


def stacked(rows):
    return jnp.concatenate([rows[:, h * HD:(h + 1) * HD] for h in range(HEADS)], axis=0)


KEY_ROWS = 256


def key_chunks(refs):
    for n, ref in enumerate(refs):
        for i in range(ref.shape[0] // KEY_ROWS):
            for side in range(2):
                rows = pl.ds(i * KEY_ROWS, KEY_ROWS)
                yield n, i, side, (ref, rows, side * 2 * HD)


def keys_of(chunk):
    ref, rows, at = chunk
    return ref[rows, at:at + HD]


def values_of(chunk):
    ref, rows, at = chunk
    return ref[rows, at + HD:at + 2 * HD]


def forward_kernel(place, q, near_own, far_own, near_sib, far_sib, out, log_total, scores):
    qs = stacked(q[...])
    lanes = HEADS * RB
    top = jnp.full((1, lanes), -jnp.inf, F32)
    chunks = [chunk for _, _, _, chunk in key_chunks((near_own, near_sib, far_own, far_sib))]
    for n, chunk in enumerate(chunks):
        got = dot(keys_of(chunk), qs, NT)
        scores[pl.ds(n * KEY_ROWS, KEY_ROWS), :] = got
        top = jnp.maximum(top, jnp.max(got, axis=0, keepdims=True))
    total = jnp.zeros((1, lanes), F32)
    acc = jnp.zeros((HD, lanes), F32)
    for n, chunk in enumerate(chunks):
        weights = jnp.exp2((scores[pl.ds(n * KEY_ROWS, KEY_ROWS), :] - top) * SCALE2)
        total = total + jnp.sum(weights, axis=0, keepdims=True)
        acc = acc + dot(values_of(chunk), weights.astype(BF), TN)
    acc = acc / total
    for h in range(HEADS):
        out[:, h * HD:(h + 1) * HD] = acc[:, h * RB:(h + 1) * RB].T.astype(BF)
    log_total[...] = top * SCALE2 + jnp.log2(total)


def backward_kernel(place, q, near_own, far_own, near_sib, far_sib, g_near, g_far, o, log_total, dq, d_own, d_sib):
    qs = stacked(q[...])
    g = plus(g_near[...], g_far[...])
    gs = stacked(g)
    lanes = HEADS * RB
    products = g.astype(F32) * o[...].astype(F32)
    delta = jnp.concatenate(
        [jnp.sum(products[:, h * HD:(h + 1) * HD].T, axis=0, keepdims=True) for h in range(HEADS)],
        axis=1,
    )
    shift = log_total[...]
    acc = jnp.zeros((HD, lanes), F32)
    for out, refs in ((d_sib, (near_sib, far_sib)), (d_own, (near_own, far_own))):
        for n, i, side, chunk in key_chunks(refs):
            keys, values = keys_of(chunk), values_of(chunk)
            probs = jnp.exp2(dot(keys, qs, NT) * SCALE2 - shift)
            dv = dot(probs.astype(BF), gs, NN).astype(BF)
            ds = (probs * (dot(values, gs, NT) - delta)).astype(BF)
            dk = (dot(ds, qs, NN) * SCALE).astype(BF)
            acc = acc + dot(keys, ds, TN)
            for t in range(KEY_ROWS // 16):
                block = n * NZ + (i * KEY_ROWS + t * 16) // 64
                at = pl.ds(((side * 4 + t % 4) * 16 + block) * 16, 16)
                out[at, :HD] = dk[t * 16:(t + 1) * 16]
                out[at, HD:] = dv[t * 16:(t + 1) * 16]
    acc = acc * SCALE
    for h in range(HEADS):
        dq[:, h * HD:(h + 1) * HD] = acc[:, h * RB:(h + 1) * RB].T.astype(BF)


def dkv_kernel(place, got, out):
    y, z = place[0], place[1]
    for n in range(2):
        side = y if n == 0 else 1 - y
        for k in range(NZ):
            block = n * NZ + k
            total = got[pl.ds(block * 16, 16), :].astype(F32)
            for d in range(1, 8):
                total = total + got[pl.ds((d * 16 + block) * 16, 16), :].astype(F32)
            slot = side * NZ + lax.rem(z + k, NZ)
            out[pl.ds(pl.multiple_of(slot * 16, 16), 16), :] = total.astype(BF)


def wo_kernel(place, o_near, o_far, og, og_sib, part_own, part_sib, cat):
    y, z, c = place[0], place[1], place[2]
    width = og.shape[1]
    for n in range(2):
        side = y if n == 0 else 1 - y
        for k in range(NZ):
            slot = side * NZ + lax.rem(z + k, NZ)
            rows = pl.ds((n * NZ + k) * RB, RB)
            cat[rows, :width] = og[pl.ds(pl.multiple_of((slot * 2 + c) * RB, RB), RB), :]
            cat[rows, width:] = og_sib[pl.ds(pl.multiple_of(slot * RB, RB), RB), :]
    size = NZ * RB
    got = dot(o_near[...], cat[:size, :], TN) + dot(o_far[...], cat[size:, :], TN)
    part_own[...] = got[:, :width].astype(BF)
    part_sib[...] = got[:, width:].astype(BF)


FIRST = (0, 7, 1, 6, 2, 5, 3)


def slots_of(place, k, owner):
    slot = lax.rem(place[1] + k, NZ)
    low = pl.multiple_of((slot * 2 + owner) * RB, RB)
    high = pl.multiple_of(((NZ + slot) * 2 + owner) * RB, RB)
    return pl.ds(low, RB), pl.ds(high, RB)


def hidden_kernel(place, hidden, w, *refs):
    blocks, grad_hidden, total = refs[:-2], refs[-2], refs[-1]
    c = place[2]
    total[...] = jnp.zeros_like(total)
    for side in range(2):
        owner = c if side == 0 else 1 - c
        for n, k in enumerate(FIRST):
            rows = blocks[side * len(FIRST) + n][...]
            low, high = slots_of(place, k, owner)
            got = dot(rows, w[...], NT).astype(BF)
            grad_hidden[low, :] = got[:RB]
            grad_hidden[high, :] = got[RB:]
            inputs = jnp.concatenate([hidden[low, :], hidden[high, :]], axis=0)
            total[...] += dot(inputs, rows, TN)


def last_kernel(place, w, up_own, down_own, up_sib, down_sib, total, hidden, before, grad_hidden, part,
                inputs, outs, in_sems, out_sems):
    c = place[2]
    places = [rows for owner in (c, 1 - c) for rows in slots_of(place, 4, owner)]
    reads = [pltpu.make_async_copy(hidden.at[rows, :], inputs.at[n], in_sems.at[n]) for n, rows in enumerate(places)]
    for read in reads:
        read.start()
    writes = []
    for n, (rows, block) in enumerate(zip(places, (up_own, down_own, up_sib, down_sib))):
        outs[n] = dot(block[...], w[...], NT).astype(BF)
        write = pltpu.make_async_copy(outs.at[n], grad_hidden.at[rows, :], out_sems.at[n])
        write.start()
        writes.append(write)
    for read in reads:
        read.wait()
    mine = jnp.concatenate([up_own[...], down_own[...], up_sib[...], down_sib[...]], axis=0)
    seen = jnp.concatenate([inputs[n] for n in range(4)], axis=0)
    part[...] = (total[...] + dot(seen, mine, TN)).astype(BF)
    for write in writes:
        write.wait()


def dp_scatter(part):
    rows, columns = part.shape
    got = lax.all_to_all(part.reshape(8, rows // 8, columns), "dp", 0, 0)
    return jnp.sum(got.astype(F32), axis=0)


SAME_CORE = [[i for i in range(32) if i % 2 == c] for c in range(2)]


def shards(queries, prefix_keys, prefix_values, hidden, out_grad, prefix_hidden, w_query, w_out):
    me = lax.axis_index("blk")
    y, z, c = me // 16, (me // 2) % 8, me % 2
    place = jnp.stack([y, z, c]).astype(jnp.int32)
    q = queries[0]
    og = out_grad[0]
    rows, width = og.shape
    hq = q.shape[1]
    half = rows // 2
    attention = HEADS * RB * rows * HD

    kv = jnp.concatenate([prefix_keys, prefix_values], axis=1)
    kv = jnp.concatenate([kv[:64], kv[64:]], axis=1)
    kv_up1, kv_down1 = send(kv, UP), send(kv, DOWN)
    given = lax.dynamic_index_in_dim(og.reshape(16, 2, RB, width), 1 - c, 1, keepdims=False)
    og_sib = send(given.reshape(half, width), SIBLING)
    w_sib = send(w_out, SIBLING)
    kv_up2, kv_down2 = send(kv_up1, UP), send(kv_down1, DOWN)

    sources = (og, og_sib, w_out, w_sib)
    chunk = bf(2 * RB, hq)
    (g4,) = call(
        functools.partial(upstream_kernel, (4,)), place, sources, (chunk,),
        flops=4 * 2 * RB * hq * width, moved=4 << 20,
    )
    up, down = call(step_a_kernel, place, (g4, kv_up2, kv_down2), (bf(RB + 64, hq),) * 2)
    a_up, a_down = send(up, UP), send(down, DOWN)
    g3, g5, g2, g6, g1, g7, g0 = call(
        functools.partial(upstream_kernel, (3, 5, 2, 6, 1, 7, 0)), place, sources + (g4,), (chunk,) * 7,
        flops=28 * 2 * RB * hq * width, moved=6 << 20, unread=1,
    )
    up, down = call(step_b_kernel, place, (a_up, a_down, g3, g5), (bf(2 * RB + 32, hq),) * 2)
    b_up, b_down = send(up, UP), send(down, DOWN)
    up, down = call(step_c_kernel, place, (b_up, b_down, g2, g6), (chunk,) * 2)
    c_up, c_down = send(up, UP), send(down, DOWN)
    (near_own,) = call(
        kv_kernel, place, (kv, kv_up1, kv_up2, kv_down1, kv_down2, a_up, a_down, b_up, b_down), (bf(512, hq),),
    )
    far_own = send(near_own, ACROSS)
    near_sib = send(near_own, SIBLING)
    up, down = call(step_c_kernel, place, (c_up, c_down, g1, g7), (chunk,) * 2)
    d_up, d_down = send(up, UP), send(down, DOWN)
    far_sib = send(far_own, SIBLING)
    g_near, g_give = call(owned_kernel, place, (g0, d_up, d_down), (bf(RB, hq),) * 2)
    g_far = send(g_give, ACROSS)

    keys = (near_own, far_own, near_sib, far_sib)
    o, log_total = call(
        forward_kernel, place, (q,) + keys, (bf(RB, hq), f32(1, HEADS * RB)),
        scratch=[pltpu.VMEM((rows, HEADS * RB), F32)],
        flops=4 * attention, moved=3 << 20, exps=HEADS * RB * rows,
    )
    dq, d_own, d_sib = call(
        backward_kernel, place, (q,) + keys + (g_near, g_far, o, log_total),
        (bf(RB, hq), bf(half, 2 * HD), bf(half, 2 * HD)),
        flops=10 * attention, moved=6 << 20, exps=HEADS * RB * rows,
    )

    o_blocks = z_gather(o)
    o_blocks[4] = jnp.concatenate(o_blocks[4])
    o_near = jnp.concatenate(o_blocks)
    o_far = send(o_near, ACROSS)

    dkv = added(d_own, send(d_sib, SIBLING))
    dkv = lax.all_to_all(dkv.reshape(8, 256, 2 * HD), "dp", 0, 0)
    (dkv,) = call(dkv_kernel, place, (dkv.reshape(half, 2 * HD),), (bf(256, 2 * HD),))
    dkv = lax.all_to_all(dkv.reshape(16, 16, 2 * HD), "blk", 0, 0, axis_index_groups=SAME_CORE)
    dkv = jnp.sum(dkv.astype(F32), axis=0).astype(BF)
    kv_low = lax.all_to_all(jnp.broadcast_to(dkv[None], (8, 16, 2 * HD)), "dp", 0, 0).reshape(RB, 2 * HD)
    columns = prefix_hidden.shape[1]
    wkv = dot(kv_low, prefix_hidden, TN).astype(BF).reshape(16, 2, 8, columns)
    wkv_got = send(lax.dynamic_index_in_dim(wkv, 1 - c, 1, keepdims=False), SIBLING)
    wkv = added(lax.dynamic_index_in_dim(wkv, c, 1, keepdims=False), wkv_got)
    wkv = lax.all_to_all(wkv, "blk", 0, 0, axis_index_groups=SAME_CORE)
    grad_wkv = jnp.sum(wkv.astype(F32), axis=0)

    dq_far = send(dq, ACROSS)
    dq_pair = jnp.where(y == 0, jnp.concatenate([dq, dq_far]), jnp.concatenate([dq_far, dq]))
    dq_blocks = z_gather(dq_pair)
    first = [dq_blocks[k] for k in FIRST]
    first_sib = [send(block, SIBLING) for block in first]
    last = list(dq_blocks[4])
    last_sib = [send(block, SIBLING) for block in last]
    grad_hidden, total = call(
        hidden_kernel, place, (hidden[0], w_query, *first, *first_sib),
        (bf(rows, width), f32(width, hq)),
        flops=3 * rows * width * hq, moved=8 << 20,
    )
    vmem, hbm = pl.BlockSpec(memory_space=pltpu.VMEM), pl.BlockSpec(memory_space=pl.ANY)
    grad_hidden, wq_part = pl.pallas_call(
        last_kernel,
        in_specs=[pl.BlockSpec(memory_space=pltpu.SMEM)] + [vmem] * 6 + [hbm] * 2,
        out_specs=(hbm, vmem),
        out_shape=(bf(rows, width), bf(width, hq)),
        scratch_shapes=[
            pltpu.VMEM((4, RB, width), BF), pltpu.VMEM((4, RB, width), BF),
            pltpu.SemaphoreType.DMA((4,)), pltpu.SemaphoreType.DMA((4,)),
        ],
        input_output_aliases={8: 0},
        compiler_params=PARAMS,
        cost_estimate=pl.CostEstimate(flops=rows * width * hq, bytes_accessed=2 << 20, transcendentals=0),
    )(place, w_query, *last, *last_sib, total, hidden[0], grad_hidden)
    grad_wq = dp_scatter(wq_part)

    wo_own, wo_sib = call(
        wo_kernel, place, (o_near, o_far, og, og_sib), (bf(hq, width), bf(hq, width)),
        scratch=[pltpu.VMEM((half, 2 * width), BF)],
        flops=2 * half * hq * 2 * width, moved=6 << 20,
    )
    wo_part = added(wo_own, send(wo_sib, SIBLING))
    grad_wo = dp_scatter(wo_part)
    return grad_hidden[None], grad_wq, grad_wo, kv_low, grad_wkv


def solution(mesh):
    in_specs = (
        P("dp", "blk", None),
        P("blk", None),
        P("blk", None),
        P("dp", None, "blk"),
        P("dp", None, "blk"),
        P("blk", "dp"),
        P("blk", None),
        P(None, "blk"),
    )
    out_specs = (
        P("dp", None, "blk"),
        P(("blk", "dp"), None),
        P("dp", "blk"),
        P("blk", None),
        P("blk", "dp"),
    )
    return jax.shard_map(shards, mesh=mesh, in_specs=in_specs, out_specs=out_specs, check_vma=False)
```

```python
import functools
import math

import jax
import jax.numpy as jnp
from jax import lax
from jax.experimental import pallas as pl
from jax.experimental.pallas import tpu as pltpu
from jax.sharding import PartitionSpec as P

BF = jnp.bfloat16
F32 = jnp.float32
NZ = 8
HEADS = 4
HD = 128
RB = 128
SCALE = HD ** -0.5
SCALE2 = SCALE * math.log2(math.e)
PARAMS = pltpu.CompilerParams(vmem_limit_bytes=56 * 1024 * 1024)

NN = (((1,), (0,)), ((), ()))
NT = (((1,), (1,)), ((), ()))
TN = (((0,), (0,)), ((), ()))


def dot(a, b, dims):
    return lax.dot_general(a, b, dims, preferred_element_type=F32)


def blk_perm(move):
    pairs = []
    for i in range(32):
        y, z, c = move(i // 16, (i // 2) % 8, i % 2)
        pairs.append((i, (y * 8 + z % 8) * 2 + c))
    return pairs


OUTWARD = blk_perm(lambda y, z, c: (y, z + 1 - 2 * c, c))
INWARD = blk_perm(lambda y, z, c: (y, z - 1 + 2 * c, c))
ACROSS = blk_perm(lambda y, z, c: (1 - y, z, c))
SIBLING = blk_perm(lambda y, z, c: (y, z, 1 - c))
Z4 = blk_perm(lambda y, z, c: (y, z ^ 4, c))
Z2 = blk_perm(lambda y, z, c: (y, z ^ 2, c))
Z1 = blk_perm(lambda y, z, c: (y, z ^ 1, c))
PIECES = [(0, 0), (1, 0), (1, 1), (2, 0), (2, 1), (3, 0), (3, 1), (4, 0)]
STARTS = [1792, 1280, 768, 256, 0]


def send(value, pairs):
    return lax.ppermute(value, "blk", pairs)


def added(*terms):
    total = terms[0].astype(F32)
    for term in terms[1:]:
        total = total + term.astype(F32)
    return total.astype(BF)


def after(value, *earlier):
    return lax.optimization_barrier((value,) + earlier)[0]


def z_gather(block, half):
    first = send(block, INWARD)
    second = send(first, INWARD)
    third = send(second, INWARD)
    return first, second, third, send(third[:half], INWARD)


def whole(count):
    return [pl.BlockSpec(memory_space=pltpu.VMEM)] * count


def away(count):
    return [pl.BlockSpec(memory_space=pl.ANY)] * count


def call(kernel, place, operands, outs, scratch=(), flops=0, moved=0, exps=0, aside=0, outs_aside=0, aliases=None):
    return pl.pallas_call(
        kernel,
        in_specs=[pl.BlockSpec(memory_space=pltpu.SMEM)] + away(aside) + whole(len(operands) - aside),
        out_specs=tuple(away(outs_aside) + whole(len(outs) - outs_aside)),
        out_shape=tuple(outs),
        scratch_shapes=list(scratch),
        input_output_aliases=aliases or {},
        compiler_params=PARAMS,
        cost_estimate=pl.CostEstimate(flops=flops, bytes_accessed=moved, transcendentals=exps),
    )(place, *operands)


def bf(*shape):
    return jax.ShapeDtypeStruct(shape, BF)


def f32(*shape):
    return jax.ShapeDtypeStruct(shape, F32)


def row_at(place, y_rel, shift, owner):
    y, z = place[0], place[1]
    side = y if y_rel == 0 else 1 - y
    slot = lax.rem(z + shift + 2 * NZ, NZ)
    return pl.ds(pl.multiple_of(((side * NZ + slot) * 2 + owner) * RB, RB), RB)


def pick_kernel(place, og, keys, values, out, kv, sems):
    c = place[2]
    toward = 2 * c - 1
    copies = []
    for y_rel in range(2):
        for j, c_rel in PIECES:
            n = len(copies)
            rows = row_at(place, y_rel, toward * j, 1 - c if c_rel == 0 else c)
            copies.append(pltpu.make_async_copy(og.at[rows, :], out.at[pl.ds(n * RB, RB), :], sems.at[n]))
            copies[-1].start()
    kv[:, :HD] = keys[...]
    kv[:, HD:] = values[...]
    for copy in copies:
        copy.wait()


def upstream_kernel(place, og, og_sib, w_own, w_sib, p4, p3, p2, p1, p0, cat, sems):
    c = place[2]
    toward = 1 - 2 * c
    width = og.shape[1]
    copies = []
    for y_rel in range(2):
        for j, c_rel in PIECES:
            n = len(copies)
            rows = row_at(place, y_rel, toward * j, c if c_rel == 0 else 1 - c)
            copies.append(pltpu.make_async_copy(og.at[rows, :], cat.at[pl.ds(n * RB, RB), pl.ds(0, width)], sems.at[n]))
            copies[-1].start()
    copies.append(pltpu.make_async_copy(og_sib, cat.at[:, pl.ds(width, width)], sems.at[16]))
    copies[-1].start()
    for copy in copies:
        copy.wait()
    outs = (p0, p1, p2, p3, p4)
    for y_rel in range(2):
        for pair in range(4):
            rows = pl.ds(y_rel * NZ * RB + pair * 2 * RB, 2 * RB)
            got = (dot(cat[rows, :width], w_own[...], NT) + dot(cat[rows, width:], w_sib[...], NT)).astype(BF)
            for n in range(2):
                j, c_rel = PIECES[pair * 2 + n]
                outs[j][pl.ds((c_rel * 2 + y_rel) * RB, RB), :] = got[n * RB:(n + 1) * RB]


def plus(a, b):
    return (a.astype(F32) + b.astype(F32)).astype(BF)


def stacked(rows):
    return jnp.concatenate([rows[:, h * HD:(h + 1) * HD] for h in range(HEADS)], axis=0)


CHUNK = 512


def forward_kernel(place, q, near_own, far_own, near_sib, far_sib, out, log_total, scores):
    qs = stacked(q[...])
    lanes = HEADS * RB
    top = jnp.full((1, lanes), -jnp.inf, F32)
    chunks = [(ref, pl.ds(i * CHUNK, CHUNK)) for ref in (near_own, near_sib, far_own, far_sib)
              for i in range(near_own.shape[0] // CHUNK)]
    for n, (ref, rows) in enumerate(chunks):
        got = dot(ref[rows, :HD], qs, NT)
        scores[pl.ds(n * CHUNK, CHUNK), :] = got
        top = jnp.maximum(top, jnp.max(got, axis=0, keepdims=True))
    total = jnp.zeros((1, lanes), F32)
    acc = jnp.zeros((HD, lanes), F32)
    for n, (ref, rows) in enumerate(chunks):
        weights = jnp.exp2((scores[pl.ds(n * CHUNK, CHUNK), :] - top) * SCALE2)
        total = total + jnp.sum(weights, axis=0, keepdims=True)
        acc = acc + dot(ref[rows, HD:], weights.astype(BF), TN)
    acc = acc / total
    for h in range(HEADS):
        out[:, h * HD:(h + 1) * HD] = acc[:, h * RB:(h + 1) * RB].T.astype(BF)
    log_total[...] = top * SCALE2 + jnp.log2(total)


def backward_kernel(place, q, near_own, far_own, near_sib, far_sib, g_near, g_far, o, log_total, dq, keep, give):
    qs = stacked(q[...])
    g = plus(g_near[...], g_far[...])
    gs = stacked(g)
    lanes = HEADS * RB
    products = g.astype(F32) * o[...].astype(F32)
    delta = jnp.concatenate(
        [jnp.sum(products[:, h * HD:(h + 1) * HD].T, axis=0, keepdims=True) for h in range(HEADS)],
        axis=1,
    )
    norm = log_total[...]
    acc = jnp.zeros((HD, lanes), F32)
    group = CHUNK // RB
    for out, refs in ((give, (near_sib, far_sib)), (keep, (near_own, far_own))):
        for y_rel, ref in enumerate(refs):
            for first in range(0, NZ, group):
                rows = pl.ds(first * RB, CHUNK)
                keys, values = ref[rows, :HD], ref[rows, HD:]
                probs = jnp.exp2(dot(keys, qs, NT) * SCALE2 - norm)
                dv = dot(probs.astype(BF), gs, NN).astype(BF)
                ds = (probs * (dot(values, gs, NT) - delta)).astype(BF)
                dk = (dot(ds, qs, NN) * SCALE).astype(BF)
                acc = acc + dot(keys, ds, TN)
                for t in range(group):
                    j, c_rel = PIECES[first + t]
                    at = pl.ds(STARTS[j] + (c_rel * 2 + y_rel) * RB, RB)
                    out[at, :HD] = dk[t * RB:(t + 1) * RB]
                    out[at, HD:] = dv[t * RB:(t + 1) * RB]
    acc = acc * SCALE
    for h in range(HEADS):
        dq[:, h * HD:(h + 1) * HD] = acc[:, h * RB:(h + 1) * RB].T.astype(BF)


def wo_kernel(place, o, o1, o2, o_last, o_first, o_second, cat, part_own, part_sib):
    width = part_own.shape[1]
    rows = jnp.concatenate([piece[...] for piece in (o, o1, o2, o_last, o_first, o_second)], axis=0)
    got = dot(rows, cat[...], TN)
    part_own[...] = got[:, :width].astype(BF)
    part_sib[...] = got[:, width:].astype(BF)


def hidden_kernel(place, hidden, w, quad, r1, r2, s1, s2, grad_hidden, total):
    c = place[2]
    toward = 1 - 2 * c
    total[...] = jnp.zeros_like(total)
    blocks = ((quad, 0, 0), (r1, 1, 0), (s1, -1, 1), (r2, 2, 0), (s2, -2, 1))
    for block, shift, owner in blocks:
        got = dot(block[...], w[...], NT).astype(BF)
        seen = []
        for n in range(4):
            mine = (n // 2 + owner) % 2 == 0
            rows = row_at(place, n % 2, toward * shift, c if mine else 1 - c)
            grad_hidden[rows, :] = got[n * RB:(n + 1) * RB]
            seen.append(hidden[rows, :])
        total[...] += dot(jnp.concatenate(seen, axis=0), block[...], TN)


def last_kernel(place, before, hidden, w, r3, s3, r4, s4, total, wo_own, wo_got, grad_hidden, parts,
                inputs, outs, in_sems, out_sems):
    c = place[2]
    toward = 1 - 2 * c
    places, mine = [], []
    for block, shift, owner in ((r3, 3, 0), (s3, -3, 1), (r4, 4, 0), (s4, 4, 1)):
        for n in range(block.shape[0] // RB):
            own = (n // 2 + owner) % 2 == 0
            places.append(row_at(place, n % 2, toward * shift, c if own else 1 - c))
    reads = [pltpu.make_async_copy(hidden.at[rows, :], inputs.at[n], in_sems.at[n]) for n, rows in enumerate(places)]
    for read in reads:
        read.start()
    writes = []
    for block in (r3, s3, r4, s4):
        got = dot(block[...], w[...], NT).astype(BF)
        for n in range(block.shape[0] // RB):
            at = len(writes)
            outs[at] = got[n * RB:(n + 1) * RB]
            writes.append(pltpu.make_async_copy(outs.at[at], grad_hidden.at[places[at], :], out_sems.at[at]))
            writes[-1].start()
    wo = plus(wo_own[...], wo_got[...])
    for d in range(8):
        parts[pl.ds(d * 128 + 64, 64), :] = wo[d * 64:(d + 1) * 64]
    for read in reads:
        read.wait()
    wq = total[...]
    at = 0
    for block in (r3, s3, r4, s4):
        count = block.shape[0] // RB
        seen = jnp.concatenate([inputs[at + n] for n in range(count)], axis=0)
        wq = wq + dot(seen, block[...], TN)
        at += count
    wq = wq.astype(BF)
    for d in range(8):
        parts[pl.ds(d * 128, 32), :] = wq[d * 32:(d + 1) * 32, :256]
        parts[pl.ds(d * 128 + 32, 32), :] = wq[d * 32:(d + 1) * 32, 256:]
    for write in writes:
        write.wait()


def shards(queries, prefix_keys, prefix_values, hidden, out_grad, prefix_hidden, w_query, w_out):
    me = lax.axis_index("blk")
    y, z, c = me // 16, (me // 2) % 8, me % 2
    place = jnp.stack([y, z, c]).astype(jnp.int32)
    q = queries[0]
    og = out_grad[0]
    rows, width = og.shape
    hq = q.shape[1]
    half = rows // 2
    attention = HEADS * RB * rows * HD

    given, kv = call(
        pick_kernel, place, (og, prefix_keys, prefix_values), (bf(half, width), bf(RB, 2 * HD)), scratch=[pltpu.SemaphoreType.DMA((16,))],
        moved=2 << 20, aside=1,
    )
    w_sib = send(w_out, SIBLING)
    og_sib = send(given, SIBLING)

    kv_pair = jnp.concatenate([kv, send(kv, SIBLING)])
    kv_first = send(kv_pair, INWARD)
    p4, p3, p2, p1, p0, og_cat = call(
        upstream_kernel, place, (og, og_sib, w_out, w_sib),
        (bf(2 * RB, hq), bf(4 * RB, hq), bf(4 * RB, hq), bf(4 * RB, hq), bf(2 * RB, hq), bf(half, 2 * width)),
        scratch=[pltpu.SemaphoreType.DMA((17,))],
        flops=4 * half * hq * width, moved=6 << 20, aside=2,
    )
    ring1 = send(p4, OUTWARD)
    kv_second = send(kv_first, INWARD)
    step = jnp.concatenate([added(p3[:2 * RB], ring1), p3[2 * RB:]])
    ring2 = send(after(step, kv_first), OUTWARD)
    kv_third = send(kv_second, INWARD)
    ring3 = send(after(added(p2, ring2), kv_second), OUTWARD)
    kv_fourth = send(kv_third[:RB], INWARD)
    near_own = jnp.concatenate((kv, kv_first, kv_second, kv_third, kv_fourth))
    far_own = send(near_own, ACROSS)
    ring4 = send(after(added(p1, ring3), near_own), OUTWARD)
    near_sib = send(near_own, SIBLING)
    far_sib = send(after(far_own, ring3), SIBLING)
    keys = (near_own, far_own, near_sib, far_sib)
    ring_sib = send(ring4[2 * RB:], SIBLING)
    g_near = added(p0[:RB], ring4[:RB], ring_sib[:RB])
    g_give = added(p0[RB:], ring4[RB:2 * RB], ring_sib[RB:])
    g_far = send(g_give, ACROSS)

    o, log_total = call(
        forward_kernel, place, (q,) + keys, (bf(RB, hq), f32(1, HEADS * RB)),
        scratch=[pltpu.VMEM((rows, HEADS * RB), F32)],
        flops=4 * attention, moved=3 << 20, exps=HEADS * RB * rows,
    )
    o_pair = jnp.concatenate([o, send(o, SIBLING)])
    dq, d_keep, d_give = call(
        backward_kernel, place, (after(q, o_pair),) + keys + (g_near, g_far, o, log_total),
        (bf(RB, hq), bf(half, 2 * HD), bf(half, 2 * HD)),
        flops=10 * attention, moved=6 << 20, exps=HEADS * RB * rows,
    )

    dkv = added(d_keep, send(d_give, SIBLING))
    t4, t3, t2, t1, t0 = (dkv[a:b] for a, b in ((0, 256), (256, 768), (768, 1280), (1280, 1792), (1792, 2048)))
    o1 = send(o_pair, INWARD)
    o2 = send(o1, INWARD)
    o3 = send(o2, INWARD)
    o4 = send(o3[:RB], INWARD)
    o_first = send(jnp.concatenate((o, o1, o2)), ACROSS)
    o_last = jnp.concatenate((o3, o4))
    turn1 = send(after(t4, o1), OUTWARD)
    dq_pair = jnp.concatenate([dq, send(dq, ACROSS)])
    quad = jnp.concatenate([dq_pair, send(dq_pair, SIBLING)])
    turn2 = send(after(jnp.concatenate([added(t3[:2 * RB], turn1), t3[2 * RB:]]), dq_pair, o2), OUTWARD)
    r1 = send(after(quad, turn1), INWARD)
    turn3 = send(after(added(t2, turn2), quad, o3), OUTWARD)
    r2 = send(r1, INWARD)
    turn4 = send(after(added(t1, turn3), r1, o_last), OUTWARD)
    r3 = send(r2, INWARD)
    turn_sib = send(after(turn4, r2, o_first)[2 * RB:], SIBLING)
    dkv_near = t0[:RB].astype(F32) + turn4[:RB].astype(F32) + turn_sib[:RB].astype(F32)
    dkv_far = send(added(t0[RB:], turn4[RB:2 * RB], turn_sib[RB:]), ACROSS)
    r4 = send(r3[:2 * RB], INWARD)
    o_second = send(after(o_last, dkv_far), ACROSS)
    dkv = (dkv_near + dkv_far.astype(F32)).astype(BF)
    s1, s2, s3, s4 = (send(block, SIBLING) for block in (r1, r2, r3, r4))
    dkv = lax.all_to_all(after(jnp.broadcast_to(dkv[None], (8, RB, 2 * HD)), r3), "dp", 0, 0)
    kv_low = jnp.sum(dkv.astype(F32), axis=0).astype(BF)

    grad_hidden, total = call(
        hidden_kernel, place, (hidden[0], w_query, quad, r1, r2, s1, s2),
        (bf(rows, width), f32(width, hq)),
        flops=3 * rows * width * hq, moved=8 << 20,
    )
    wo_own, wo_give = call(
        wo_kernel, place, (o, o1, o2, o_last, o_first, o_second, og_cat), (bf(hq, width), bf(hq, width)),
        flops=2 * half * hq * 2 * width, moved=5 << 20,
    )
    wo_got = send(wo_give, SIBLING)

    columns = prefix_hidden.shape[1]
    kv_cols = kv_low.T.reshape(2, 2, 2, 2, 2, 8, RB)
    for axis, bit in enumerate((y, z // 4, z // 2 % 2, z % 2, c)):
        kv_cols = jnp.where(bit == 1, jnp.flip(kv_cols, axis), kv_cols)
    kv_cols = jnp.transpose(kv_cols, (4, 0, 1, 2, 3, 5, 6)).reshape(2 * HD, RB)
    wkv = dot(after(kv_cols, total, wo_own, r4), prefix_hidden, NN).astype(BF)
    grad_hidden, parts = call(
        last_kernel, place, (grad_hidden, hidden[0], w_query, r3, s3, r4, s4, total, wo_own, wo_got),
        (bf(rows, width), bf(1024, 256)),
        scratch=[
            pltpu.VMEM((12, RB, width), BF), pltpu.VMEM((12, RB, width), BF),
            pltpu.SemaphoreType.DMA((12,)), pltpu.SemaphoreType.DMA((12,)),
        ],
        flops=rows * width * hq, moved=3 << 20, aside=2, outs_aside=1, aliases={1: 0},
    )
    for pairs, earlier in ((SIBLING, r4), (ACROSS, r4), (Z4, parts), (Z2, parts), (Z1, parts)):
        size = wkv.shape[0] // 2
        got = send(after(wkv, earlier)[size:], pairs)
        wkv = added(wkv[:size], got) if size > 8 else wkv[:size].astype(F32) + got.astype(F32)
    grad_wkv = wkv
    parts = lax.all_to_all(parts.reshape(8, 128, 256), "dp", 0, 0)
    sums = jnp.sum(parts.astype(F32), axis=0)
    grad_wq = jnp.concatenate([sums[:32], sums[32:64]], axis=1)
    return grad_hidden[None], grad_wq, sums[64:], kv_low, grad_wkv


def solution(mesh):
    in_specs = (
        P("dp", "blk", None),
        P("blk", None),
        P("blk", None),
        P("dp", None, "blk"),
        P("dp", None, "blk"),
        P("blk", "dp"),
        P("blk", None),
        P(None, "blk"),
    )
    out_specs = (
        P("dp", None, "blk"),
        P(("blk", "dp"), None),
        P("dp", "blk"),
        P("blk", None),
        P("blk", "dp"),
    )
    return jax.shard_map(shards, mesh=mesh, in_specs=in_specs, out_specs=out_specs, check_vma=False)
```

```python
import functools
import math

import jax
import jax.numpy as jnp
from jax import lax
from jax.experimental import pallas as pl
from jax.experimental.pallas import tpu as pltpu
from jax.sharding import PartitionSpec as P

BF = jnp.bfloat16
F32 = jnp.float32
NZ = 8
HEADS = 4
HD = 128
RB = 128
SCALE = HD ** -0.5
SCALE2 = SCALE * math.log2(math.e)
PARAMS = pltpu.CompilerParams(vmem_limit_bytes=56 * 1024 * 1024)

NN = (((1,), (0,)), ((), ()))
NT = (((1,), (1,)), ((), ()))
TN = (((0,), (0,)), ((), ()))


def dot(a, b, dims):
    return lax.dot_general(a, b, dims, preferred_element_type=F32)


def blk_perm(move):
    pairs = []
    for i in range(32):
        y, z, c = move(i // 16, (i // 2) % 8, i % 2)
        pairs.append((i, (y * 8 + z % 8) * 2 + c))
    return pairs


OUTWARD = blk_perm(lambda y, z, c: (y, z + 1 - 2 * c, c))
INWARD = blk_perm(lambda y, z, c: (y, z - 1 + 2 * c, c))
ACROSS = blk_perm(lambda y, z, c: (1 - y, z, c))
SIBLING = blk_perm(lambda y, z, c: (y, z, 1 - c))
Z4 = blk_perm(lambda y, z, c: (y, z ^ 4, c))
Z2 = blk_perm(lambda y, z, c: (y, z ^ 2, c))
Z1 = blk_perm(lambda y, z, c: (y, z ^ 1, c))
DP_X1 = [(i, i ^ 1) for i in range(8)]
DP_X2 = [(i, i ^ 2) for i in range(8)]
DP_Y = [(i, i ^ 4) for i in range(8)]
PIECES = [(0, 0), (1, 0), (1, 1), (2, 0), (2, 1), (3, 0), (3, 1), (4, 0)]
STARTS = [1792, 1280, 768, 256, 0]


def send(value, pairs):
    return lax.ppermute(value, "blk", pairs)


def added(*terms):
    total = terms[0].astype(F32)
    for term in terms[1:]:
        total = total + term.astype(F32)
    return total.astype(BF)


def after(value, *earlier):
    return lax.optimization_barrier((value,) + earlier)[0]


def z_gather(block, half):
    first = send(block, INWARD)
    second = send(first, INWARD)
    third = send(second, INWARD)
    return first, second, third, send(third[:half], INWARD)


def whole(count):
    return [pl.BlockSpec(memory_space=pltpu.VMEM)] * count


def away(count):
    return [pl.BlockSpec(memory_space=pl.ANY)] * count


def call(kernel, place, operands, outs, scratch=(), flops=0, moved=0, exps=0, aside=0, outs_aside=0, aliases=None):
    return pl.pallas_call(
        kernel,
        in_specs=[pl.BlockSpec(memory_space=pltpu.SMEM)] + away(aside) + whole(len(operands) - aside),
        out_specs=tuple(away(outs_aside) + whole(len(outs) - outs_aside)),
        out_shape=tuple(outs),
        scratch_shapes=list(scratch),
        input_output_aliases=aliases or {},
        compiler_params=PARAMS,
        cost_estimate=pl.CostEstimate(flops=flops, bytes_accessed=moved, transcendentals=exps),
    )(place, *operands)


def bf(*shape):
    return jax.ShapeDtypeStruct(shape, BF)


def f32(*shape):
    return jax.ShapeDtypeStruct(shape, F32)


def row_at(place, y_rel, shift, owner):
    y, z = place[0], place[1]
    side = y if y_rel == 0 else 1 - y
    slot = lax.rem(z + shift + 2 * NZ, NZ)
    return pl.ds(pl.multiple_of(((side * NZ + slot) * 2 + owner) * RB, RB), RB)


def pick_kernel(place, og, keys, values, out, kv, sems):
    c = place[2]
    toward = 2 * c - 1
    copies = []
    for y_rel in range(2):
        for j, c_rel in PIECES:
            n = len(copies)
            rows = row_at(place, y_rel, toward * j, 1 - c if c_rel == 0 else c)
            copies.append(pltpu.make_async_copy(og.at[rows, :], out.at[pl.ds(n * RB, RB), :], sems.at[n]))
            copies[-1].start()
    kv[:, :HD] = keys[...]
    kv[:, HD:] = values[...]
    for copy in copies:
        copy.wait()


def upstream_kernel(place, og, og_sib, w_own, w_sib, p4, p3, p2, p1, p0, cat, sems):
    c = place[2]
    toward = 1 - 2 * c
    width = og.shape[1]
    copies = []
    for y_rel in range(2):
        for j, c_rel in PIECES:
            n = len(copies)
            rows = row_at(place, y_rel, toward * j, c if c_rel == 0 else 1 - c)
            copies.append(pltpu.make_async_copy(og.at[rows, :], cat.at[pl.ds(n * RB, RB), pl.ds(0, width)], sems.at[n]))
            copies[-1].start()
    copies.append(pltpu.make_async_copy(og_sib, cat.at[:, pl.ds(width, width)], sems.at[16]))
    copies[-1].start()
    for copy in copies:
        copy.wait()
    outs = (p0, p1, p2, p3, p4)
    for y_rel in range(2):
        for pair in range(4):
            rows = pl.ds(y_rel * NZ * RB + pair * 2 * RB, 2 * RB)
            got = (dot(cat[rows, :width], w_own[...], NT) + dot(cat[rows, width:], w_sib[...], NT)).astype(BF)
            for n in range(2):
                j, c_rel = PIECES[pair * 2 + n]
                outs[j][pl.ds((c_rel * 2 + y_rel) * RB, RB), :] = got[n * RB:(n + 1) * RB]


def plus(a, b):
    return (a.astype(F32) + b.astype(F32)).astype(BF)


def stacked(rows):
    return jnp.concatenate([rows[:, h * HD:(h + 1) * HD] for h in range(HEADS)], axis=0)


CHUNK = 512


def forward_kernel(place, q, near_own, far_own, near_sib, far_sib, out, log_total, scores):
    qs = stacked(q[...])
    lanes = HEADS * RB
    top = jnp.full((1, lanes), -jnp.inf, F32)
    chunks = [(ref, pl.ds(i * CHUNK, CHUNK)) for ref in (near_own, near_sib, far_own, far_sib)
              for i in range(near_own.shape[0] // CHUNK)]
    for n, (ref, rows) in enumerate(chunks):
        got = dot(ref[rows, :HD], qs, NT)
        scores[pl.ds(n * CHUNK, CHUNK), :] = got
        top = jnp.maximum(top, jnp.max(got, axis=0, keepdims=True))
    total = jnp.zeros((1, lanes), F32)
    acc = jnp.zeros((HD, lanes), F32)
    for n, (ref, rows) in enumerate(chunks):
        weights = jnp.exp2((scores[pl.ds(n * CHUNK, CHUNK), :] - top) * SCALE2)
        total = total + jnp.sum(weights, axis=0, keepdims=True)
        acc = acc + dot(ref[rows, HD:], weights.astype(BF), TN)
    acc = acc / total
    for h in range(HEADS):
        out[:, h * HD:(h + 1) * HD] = acc[:, h * RB:(h + 1) * RB].T.astype(BF)
    log_total[...] = top * SCALE2 + jnp.log2(total)


def backward_kernel(place, q, near_own, far_own, near_sib, far_sib, g_near, g_far, o, log_total, dq, keep, give):
    qs = stacked(q[...])
    g = plus(g_near[...], g_far[...])
    gs = stacked(g)
    lanes = HEADS * RB
    products = g.astype(F32) * o[...].astype(F32)
    delta = jnp.concatenate(
        [jnp.sum(products[:, h * HD:(h + 1) * HD].T, axis=0, keepdims=True) for h in range(HEADS)],
        axis=1,
    )
    norm = log_total[...]
    acc = jnp.zeros((HD, lanes), F32)
    group = CHUNK // RB
    for out, refs in ((give, (near_sib, far_sib)), (keep, (near_own, far_own))):
        for y_rel, ref in enumerate(refs):
            for first in range(0, NZ, group):
                rows = pl.ds(first * RB, CHUNK)
                keys, values = ref[rows, :HD], ref[rows, HD:]
                probs = jnp.exp2(dot(keys, qs, NT) * SCALE2 - norm)
                dv = dot(probs.astype(BF), gs, NN).astype(BF)
                ds = (probs * (dot(values, gs, NT) - delta)).astype(BF)
                dk = (dot(ds, qs, NN) * SCALE).astype(BF)
                acc = acc + dot(keys, ds, TN)
                for t in range(group):
                    j, c_rel = PIECES[first + t]
                    at = pl.ds(STARTS[j] + (c_rel * 2 + y_rel) * RB, RB)
                    out[at, :HD] = dk[t * RB:(t + 1) * RB]
                    out[at, HD:] = dv[t * RB:(t + 1) * RB]
    acc = acc * SCALE
    for h in range(HEADS):
        dq[:, h * HD:(h + 1) * HD] = acc[:, h * RB:(h + 1) * RB].T.astype(BF)


def wo_kernel(place, o, o1, o2, o_last, o_first, o_second, cat, part_own, part_sib):
    width = part_own.shape[1]
    rows = jnp.concatenate([piece[...] for piece in (o, o1, o2, o_last, o_first, o_second)], axis=0)
    got = dot(rows, cat[...], TN)
    part_own[...] = got[:, :width].astype(BF)
    part_sib[...] = got[:, width:].astype(BF)


def hidden_kernel(place, hidden, w, quad, r1, s1, grad_hidden, total):
    c = place[2]
    toward = 1 - 2 * c
    total[...] = jnp.zeros_like(total)
    blocks = ((quad, 0, 0), (r1, 1, 0), (s1, -1, 1))
    for block, shift, owner in blocks:
        got = dot(block[...], w[...], NT).astype(BF)
        seen = []
        for n in range(4):
            mine = (n // 2 + owner) % 2 == 0
            rows = row_at(place, n % 2, toward * shift, c if mine else 1 - c)
            grad_hidden[rows, :] = got[n * RB:(n + 1) * RB]
            seen.append(hidden[rows, :])
        total[...] += dot(jnp.concatenate(seen, axis=0), block[...], TN)


def last_kernel(place, before, hidden, w, r2, s2, r3, s3, r4, s4, total, wo_own, wo_got, grad_hidden, parts,
                inputs, outs, in_sems, out_sems):
    c = place[2]
    toward = 1 - 2 * c
    places, mine = [], []
    for block, shift, owner in ((r2, 2, 0), (s2, -2, 1), (r3, 3, 0), (s3, -3, 1), (r4, 4, 0), (s4, 4, 1)):
        for n in range(block.shape[0] // RB):
            own = (n // 2 + owner) % 2 == 0
            places.append(row_at(place, n % 2, toward * shift, c if own else 1 - c))
    reads = [pltpu.make_async_copy(hidden.at[rows, :], inputs.at[n], in_sems.at[n]) for n, rows in enumerate(places)]
    for read in reads:
        read.start()
    writes = []
    for block in (r2, s2, r3, s3, r4, s4):
        got = dot(block[...], w[...], NT).astype(BF)
        for n in range(block.shape[0] // RB):
            at = len(writes)
            outs[at] = got[n * RB:(n + 1) * RB]
            writes.append(pltpu.make_async_copy(outs.at[at], grad_hidden.at[places[at], :], out_sems.at[at]))
            writes[-1].start()
    wo = plus(wo_own[...], wo_got[...])
    for d in range(8):
        parts[pl.ds(d * 128 + 64, 64), :] = wo[d * 64:(d + 1) * 64]
    for read in reads:
        read.wait()
    wq = total[...]
    at = 0
    for block in (r2, s2, r3, s3, r4, s4):
        count = block.shape[0] // RB
        seen = jnp.concatenate([inputs[at + n] for n in range(count)], axis=0)
        wq = wq + dot(seen, block[...], TN)
        at += count
    wq = wq.astype(BF)
    for d in range(8):
        parts[pl.ds(d * 128, 32), :] = wq[d * 32:(d + 1) * 32, :256]
        parts[pl.ds(d * 128 + 32, 32), :] = wq[d * 32:(d + 1) * 32, 256:]
    for write in writes:
        write.wait()


def shards(queries, prefix_keys, prefix_values, hidden, out_grad, prefix_hidden, w_query, w_out):
    me = lax.axis_index("blk")
    y, z, c = me // 16, (me // 2) % 8, me % 2
    place = jnp.stack([y, z, c]).astype(jnp.int32)
    q = queries[0]
    og = out_grad[0]
    rows, width = og.shape
    hq = q.shape[1]
    half = rows // 2
    attention = HEADS * RB * rows * HD

    given, kv = call(
        pick_kernel, place, (og, prefix_keys, prefix_values), (bf(half, width), bf(RB, 2 * HD)), scratch=[pltpu.SemaphoreType.DMA((16,))],
        moved=2 << 20, aside=1,
    )
    w_sib = send(w_out, SIBLING)
    og_sib = send(given, SIBLING)

    kv_pair = jnp.concatenate([kv, send(kv, SIBLING)])
    kv_first = send(kv_pair, INWARD)
    p4, p3, p2, p1, p0, og_cat = call(
        upstream_kernel, place, (og, og_sib, w_out, w_sib),
        (bf(2 * RB, hq), bf(4 * RB, hq), bf(4 * RB, hq), bf(4 * RB, hq), bf(2 * RB, hq), bf(half, 2 * width)),
        scratch=[pltpu.SemaphoreType.DMA((17,))],
        flops=4 * half * hq * width, moved=6 << 20, aside=2,
    )
    ring1 = send(p4, OUTWARD)
    kv_second = send(kv_first, INWARD)
    step = jnp.concatenate([added(p3[:2 * RB], ring1), p3[2 * RB:]])
    ring2 = send(after(step, kv_first), OUTWARD)
    kv_third = send(kv_second, INWARD)
    ring3 = send(after(added(p2, ring2), kv_second), OUTWARD)
    kv_fourth = send(kv_third[:RB], INWARD)
    near_own = jnp.concatenate((kv, kv_first, kv_second, kv_third, kv_fourth))
    far_own = send(near_own, ACROSS)
    ring4 = send(after(added(p1, ring3), near_own), OUTWARD)
    near_sib = send(near_own, SIBLING)
    far_sib = send(after(far_own, ring3), SIBLING)
    keys = (near_own, far_own, near_sib, far_sib)
    ring_sib = send(ring4[2 * RB:], SIBLING)
    g_near = added(p0[:RB], ring4[:RB], ring_sib[:RB])
    g_give = added(p0[RB:], ring4[RB:2 * RB], ring_sib[RB:])
    g_far = send(g_give, ACROSS)

    o, log_total = call(
        forward_kernel, place, (q,) + keys, (bf(RB, hq), f32(1, HEADS * RB)),
        scratch=[pltpu.VMEM((rows, HEADS * RB), F32)],
        flops=4 * attention, moved=3 << 20, exps=HEADS * RB * rows,
    )
    dq, d_keep, d_give = call(
        backward_kernel, place, (q,) + keys + (g_near, g_far, o, log_total),
        (bf(RB, hq), bf(half, 2 * HD), bf(half, 2 * HD)),
        flops=10 * attention, moved=6 << 20, exps=HEADS * RB * rows,
    )

    dkv = added(d_keep, send(d_give, SIBLING))
    t4, t3, t2, t1, t0 = (dkv[a:b] for a, b in ((0, 256), (256, 768), (768, 1280), (1280, 1792), (1792, 2048)))
    o_pair = jnp.concatenate([o, send(after(o, dq), SIBLING)])
    o1 = send(o_pair, INWARD)
    turn1 = send(t4, OUTWARD)
    o2 = send(after(o1, turn1), INWARD)
    o_first = send(jnp.concatenate((o, o1, o2)), ACROSS)
    dq_pair = jnp.concatenate([dq, send(dq, ACROSS)])
    quad = jnp.concatenate([dq_pair, send(dq_pair, SIBLING)])
    turn2 = send(after(jnp.concatenate([added(t3[:2 * RB], turn1), t3[2 * RB:]]), dq_pair), OUTWARD)
    o3 = send(after(o2, turn2), INWARD)
    r1 = send(after(quad, turn1), INWARD)
    turn3 = send(after(added(t2, turn2), quad), OUTWARD)
    r2 = send(r1, INWARD)
    o4 = send(after(o3[:RB], turn3), INWARD)
    o_last = jnp.concatenate((o3, o4))
    turn4 = send(after(added(t1, turn3), r1), OUTWARD)
    r3 = send(r2, INWARD)
    s1 = send(r1, SIBLING)
    grad_hidden, total = call(
        hidden_kernel, place, (hidden[0], w_query, quad, r1, s1),
        (bf(rows, width), f32(width, hq)),
        flops=3 * rows * width * hq, moved=8 << 20,
    )
    turn_sib = send(after(turn4, r2, o_first, total)[2 * RB:], SIBLING)
    dkv_near = t0[:RB].astype(F32) + turn4[:RB].astype(F32) + turn_sib[:RB].astype(F32)
    dkv_far = send(added(t0[RB:], turn4[RB:2 * RB], turn_sib[RB:]), ACROSS)
    r4 = send(r3[:2 * RB], INWARD)
    o_second = send(after(o_last, dkv_far), ACROSS)
    dkv = (dkv_near + dkv_far.astype(F32)).astype(BF)
    s2, s3, s4 = (send(block, SIBLING) for block in (r2, r3, r4))
    dkv = after(dkv, r3)
    for pairs in (DP_X1, DP_X2, DP_Y):
        dkv = added(dkv, lax.ppermute(dkv, "dp", pairs))
    kv_low = dkv

    wo_own, wo_give = call(
        wo_kernel, place, (o, o1, o2, o_last, o_first, o_second, og_cat), (bf(hq, width), bf(hq, width)),
        flops=2 * half * hq * 2 * width, moved=5 << 20,
    )
    wo_got = send(wo_give, SIBLING)

    columns = prefix_hidden.shape[1]
    kv_cols = kv_low.T.reshape(2, 2, 2, 2, 2, 8, RB)
    for axis, bit in enumerate((y, z // 4, z // 2 % 2, z % 2, c)):
        kv_cols = jnp.where(bit == 1, jnp.flip(kv_cols, axis), kv_cols)
    kv_cols = jnp.transpose(kv_cols, (4, 1, 0, 2, 3, 5, 6)).reshape(2 * HD, RB)
    wkv = dot(after(kv_cols, wo_own, r4), prefix_hidden, NN).astype(BF)
    grad_hidden, parts = call(
        last_kernel, place, (grad_hidden, hidden[0], w_query, r2, s2, r3, s3, r4, s4, total, wo_own, wo_got),
        (bf(rows, width), bf(1024, 256)),
        scratch=[
            pltpu.VMEM((20, RB, width), BF), pltpu.VMEM((20, RB, width), BF),
            pltpu.SemaphoreType.DMA((20,)), pltpu.SemaphoreType.DMA((20,)),
        ],
        flops=rows * width * hq, moved=3 << 20, aside=2, outs_aside=1, aliases={1: 0},
    )
    for pairs, earlier in ((SIBLING, r4), (Z4, r4), (ACROSS, parts), (Z2, parts), (Z1, parts)):
        size = wkv.shape[0] // 2
        got = send(after(wkv, earlier)[size:], pairs)
        wkv = added(wkv[:size], got) if size > 8 else wkv[:size].astype(F32) + got.astype(F32)
    grad_wkv = wkv
    parts = lax.all_to_all(parts.reshape(8, 128, 256), "dp", 0, 0)
    sums = jnp.sum(parts.astype(F32), axis=0)
    grad_wq = jnp.concatenate([sums[:32], sums[32:64]], axis=1)
    return grad_hidden[None], grad_wq, sums[64:], kv_low, grad_wkv


def solution(mesh):
    in_specs = (
        P("dp", "blk", None),
        P("blk", None),
        P("blk", None),
        P("dp", None, "blk"),
        P("dp", None, "blk"),
        P("blk", "dp"),
        P("blk", None),
        P(None, "blk"),
    )
    out_specs = (
        P("dp", None, "blk"),
        P(("blk", "dp"), None),
        P("dp", "blk"),
        P("blk", None),
        P("blk", "dp"),
    )
    return jax.shard_map(shards, mesh=mesh, in_specs=in_specs, out_specs=out_specs, check_vma=False)
```

```python
import functools
import math

import jax
import jax.numpy as jnp
from jax import lax
from jax.experimental import pallas as pl
from jax.experimental.pallas import tpu as pltpu
from jax.sharding import PartitionSpec as P

BF = jnp.bfloat16
F32 = jnp.float32
NZ = 8
HEADS = 4
HD = 128
RB = 128
SCALE = HD ** -0.5
SCALE2 = SCALE * math.log2(math.e)
PARAMS = pltpu.CompilerParams(vmem_limit_bytes=56 * 1024 * 1024)

NN = (((1,), (0,)), ((), ()))
NT = (((1,), (1,)), ((), ()))
TN = (((0,), (0,)), ((), ()))


def dot(a, b, dims):
    return lax.dot_general(a, b, dims, preferred_element_type=F32)


def blk_perm(move):
    pairs = []
    for i in range(32):
        y, z, c = move(i // 16, (i // 2) % 8, i % 2)
        pairs.append((i, (y * 8 + z % 8) * 2 + c))
    return pairs


OUTWARD = blk_perm(lambda y, z, c: (y, z + 1 - 2 * c, c))
INWARD = blk_perm(lambda y, z, c: (y, z - 1 + 2 * c, c))
ACROSS = blk_perm(lambda y, z, c: (1 - y, z, c))
SIBLING = blk_perm(lambda y, z, c: (y, z, 1 - c))
Z4 = blk_perm(lambda y, z, c: (y, z ^ 4, c))
Z2 = blk_perm(lambda y, z, c: (y, z ^ 2, c))
Z1 = blk_perm(lambda y, z, c: (y, z ^ 1, c))
DP_X1 = [(i, i ^ 1) for i in range(8)]
DP_X2 = [(i, i ^ 2) for i in range(8)]
DP_Y = [(i, i ^ 4) for i in range(8)]
PIECES = [(0, 0), (1, 0), (1, 1), (2, 0), (2, 1), (3, 0), (3, 1), (4, 0)]
STARTS = [1792, 1280, 768, 256, 0]


def send(value, pairs):
    return lax.ppermute(value, "blk", pairs)


def added(*terms):
    total = terms[0].astype(F32)
    for term in terms[1:]:
        total = total + term.astype(F32)
    return total.astype(BF)


def after(value, *earlier):
    return lax.optimization_barrier((value,) + earlier)[0]


def z_gather(block, half):
    first = send(block, INWARD)
    second = send(first, INWARD)
    third = send(second, INWARD)
    return first, second, third, send(third[:half], INWARD)


def whole(count):
    return [pl.BlockSpec(memory_space=pltpu.VMEM)] * count


def away(count):
    return [pl.BlockSpec(memory_space=pl.ANY)] * count


def call(kernel, place, operands, outs, scratch=(), flops=0, moved=0, exps=0, aside=0, outs_aside=0, aliases=None):
    return pl.pallas_call(
        kernel,
        in_specs=[pl.BlockSpec(memory_space=pltpu.SMEM)] + away(aside) + whole(len(operands) - aside),
        out_specs=tuple(away(outs_aside) + whole(len(outs) - outs_aside)),
        out_shape=tuple(outs),
        scratch_shapes=list(scratch),
        input_output_aliases=aliases or {},
        compiler_params=PARAMS,
        cost_estimate=pl.CostEstimate(flops=flops, bytes_accessed=moved, transcendentals=exps),
    )(place, *operands)


def bf(*shape):
    return jax.ShapeDtypeStruct(shape, BF)


def f32(*shape):
    return jax.ShapeDtypeStruct(shape, F32)


def row_at(place, y_rel, shift, owner):
    y, z = place[0], place[1]
    side = y if y_rel == 0 else 1 - y
    slot = lax.rem(z + shift + 2 * NZ, NZ)
    return pl.ds(pl.multiple_of(((side * NZ + slot) * 2 + owner) * RB, RB), RB)


def pick_kernel(place, og, keys, values, out, kv, sems):
    c = place[2]
    toward = 2 * c - 1
    copies = []
    for y_rel in range(2):
        for j, c_rel in PIECES:
            n = len(copies)
            rows = row_at(place, y_rel, toward * j, 1 - c if c_rel == 0 else c)
            copies.append(pltpu.make_async_copy(og.at[rows, :], out.at[pl.ds(n * RB, RB), :], sems.at[n]))
            copies[-1].start()
    kv[:, :HD] = keys[...]
    kv[:, HD:] = values[...]
    for copy in copies:
        copy.wait()


def upstream_kernel(place, og, og_sib, w_own, w_sib, p4, p3, p2, p1, p0, cat, sems):
    c = place[2]
    toward = 1 - 2 * c
    width = og.shape[1]
    copies = []
    for y_rel in range(2):
        for j, c_rel in PIECES:
            n = len(copies)
            rows = row_at(place, y_rel, toward * j, c if c_rel == 0 else 1 - c)
            copies.append(pltpu.make_async_copy(og.at[rows, :], cat.at[pl.ds(n * RB, RB), pl.ds(0, width)], sems.at[n]))
            copies[-1].start()
    copies.append(pltpu.make_async_copy(og_sib, cat.at[:, pl.ds(width, width)], sems.at[16]))
    copies[-1].start()
    for copy in copies:
        copy.wait()
    outs = (p0, p1, p2, p3, p4)
    for y_rel in range(2):
        for pair in range(4):
            rows = pl.ds(y_rel * NZ * RB + pair * 2 * RB, 2 * RB)
            got = (dot(cat[rows, :width], w_own[...], NT) + dot(cat[rows, width:], w_sib[...], NT)).astype(BF)
            for n in range(2):
                j, c_rel = PIECES[pair * 2 + n]
                outs[j][pl.ds((c_rel * 2 + y_rel) * RB, RB), :] = got[n * RB:(n + 1) * RB]


def plus(a, b):
    return (a.astype(F32) + b.astype(F32)).astype(BF)


def stacked(rows):
    return jnp.concatenate([rows[:, h * HD:(h + 1) * HD] for h in range(HEADS)], axis=0)


CHUNK = 512


def forward_kernel(place, q, near_own, far_own, near_sib, far_sib, out, log_total, scores):
    qs = stacked(q[...])
    lanes = HEADS * RB
    top = jnp.full((1, lanes), -jnp.inf, F32)
    chunks = [(ref, pl.ds(i * CHUNK, CHUNK)) for ref in (near_own, near_sib, far_own, far_sib)
              for i in range(near_own.shape[0] // CHUNK)]
    for n, (ref, rows) in enumerate(chunks):
        got = dot(ref[rows, :HD], qs, NT)
        scores[pl.ds(n * CHUNK, CHUNK), :] = got
        top = jnp.maximum(top, jnp.max(got, axis=0, keepdims=True))
    total = jnp.zeros((1, lanes), F32)
    acc = jnp.zeros((HD, lanes), F32)
    for n, (ref, rows) in enumerate(chunks):
        weights = jnp.exp2((scores[pl.ds(n * CHUNK, CHUNK), :] - top) * SCALE2)
        total = total + jnp.sum(weights, axis=0, keepdims=True)
        acc = acc + dot(ref[rows, HD:], weights.astype(BF), TN)
    acc = acc / total
    for h in range(HEADS):
        out[:, h * HD:(h + 1) * HD] = acc[:, h * RB:(h + 1) * RB].T.astype(BF)
    log_total[...] = top * SCALE2 + jnp.log2(total)


def backward_kernel(place, q, near_own, far_own, near_sib, far_sib, g_near, g_far, o, log_total, dq, keep, give):
    qs = stacked(q[...])
    g = plus(g_near[...], g_far[...])
    gs = stacked(g)
    lanes = HEADS * RB
    products = g.astype(F32) * o[...].astype(F32)
    delta = jnp.concatenate(
        [jnp.sum(products[:, h * HD:(h + 1) * HD].T, axis=0, keepdims=True) for h in range(HEADS)],
        axis=1,
    )
    norm = log_total[...]
    acc = jnp.zeros((HD, lanes), F32)
    group = CHUNK // RB
    for out, refs in ((give, (near_sib, far_sib)), (keep, (near_own, far_own))):
        for y_rel, ref in enumerate(refs):
            for first in range(0, NZ, group):
                rows = pl.ds(first * RB, CHUNK)
                keys, values = ref[rows, :HD], ref[rows, HD:]
                probs = jnp.exp2(dot(keys, qs, NT) * SCALE2 - norm)
                dv = dot(probs.astype(BF), gs, NN).astype(BF)
                ds = (probs * (dot(values, gs, NT) - delta)).astype(BF)
                dk = (dot(ds, qs, NN) * SCALE).astype(BF)
                acc = acc + dot(keys, ds, TN)
                for t in range(group):
                    j, c_rel = PIECES[first + t]
                    at = pl.ds(STARTS[j] + (c_rel * 2 + y_rel) * RB, RB)
                    out[at, :HD] = dk[t * RB:(t + 1) * RB]
                    out[at, HD:] = dv[t * RB:(t + 1) * RB]
    acc = acc * SCALE
    for h in range(HEADS):
        dq[:, h * HD:(h + 1) * HD] = acc[:, h * RB:(h + 1) * RB].T.astype(BF)


def wo_kernel(place, o, o1, o2, o_last, o_first, o_second, cat, part_own, part_sib):
    width = part_own.shape[1]
    rows = jnp.concatenate([piece[...] for piece in (o, o1, o2, o_last, o_first, o_second)], axis=0)
    got = dot(rows, cat[...], TN)
    part_own[...] = got[:, :width].astype(BF)
    part_sib[...] = got[:, width:].astype(BF)


def hidden_kernel(place, hidden, w, quad, r1, s1, grad_hidden, total):
    c = place[2]
    toward = 1 - 2 * c
    total[...] = jnp.zeros_like(total)
    blocks = ((quad, 0, 0), (r1, 1, 0), (s1, -1, 1))
    for block, shift, owner in blocks:
        got = dot(block[...], w[...], NT).astype(BF)
        seen = []
        for n in range(4):
            mine = (n // 2 + owner) % 2 == 0
            rows = row_at(place, n % 2, toward * shift, c if mine else 1 - c)
            grad_hidden[rows, :] = got[n * RB:(n + 1) * RB]
            seen.append(hidden[rows, :])
        total[...] += dot(jnp.concatenate(seen, axis=0), block[...], TN)


def last_kernel(place, before, hidden, w, r2, s2, r3, s3, r4, s4, total, wo_own, wo_got, grad_hidden, parts,
                inputs, outs, in_sems, out_sems):
    c = place[2]
    toward = 1 - 2 * c
    places, mine = [], []
    for block, shift, owner in ((r2, 2, 0), (s2, -2, 1), (r3, 3, 0), (s3, -3, 1), (r4, 4, 0), (s4, 4, 1)):
        for n in range(block.shape[0] // RB):
            own = (n // 2 + owner) % 2 == 0
            places.append(row_at(place, n % 2, toward * shift, c if own else 1 - c))
    reads = [pltpu.make_async_copy(hidden.at[rows, :], inputs.at[n], in_sems.at[n]) for n, rows in enumerate(places)]
    for read in reads:
        read.start()
    writes = []
    for block in (r2, s2, r3, s3, r4, s4):
        got = dot(block[...], w[...], NT).astype(BF)
        for n in range(block.shape[0] // RB):
            at = len(writes)
            outs[at] = got[n * RB:(n + 1) * RB]
            writes.append(pltpu.make_async_copy(outs.at[at], grad_hidden.at[places[at], :], out_sems.at[at]))
            writes[-1].start()
    wo = plus(wo_own[...], wo_got[...])
    for d in range(8):
        parts[pl.ds(d * 128 + 64, 64), :] = wo[d * 64:(d + 1) * 64]
    for read in reads:
        read.wait()
    wq = total[...]
    at = 0
    for block in (r2, s2, r3, s3, r4, s4):
        count = block.shape[0] // RB
        seen = jnp.concatenate([inputs[at + n] for n in range(count)], axis=0)
        wq = wq + dot(seen, block[...], TN)
        at += count
    wq = wq.astype(BF)
    for d in range(8):
        parts[pl.ds(d * 128, 32), :] = wq[d * 32:(d + 1) * 32, :256]
        parts[pl.ds(d * 128 + 32, 32), :] = wq[d * 32:(d + 1) * 32, 256:]
    for write in writes:
        write.wait()


def shards(queries, prefix_keys, prefix_values, hidden, out_grad, prefix_hidden, w_query, w_out):
    me = lax.axis_index("blk")
    y, z, c = me // 16, (me // 2) % 8, me % 2
    place = jnp.stack([y, z, c]).astype(jnp.int32)
    q = queries[0]
    og = out_grad[0]
    rows, width = og.shape
    hq = q.shape[1]
    half = rows // 2
    attention = HEADS * RB * rows * HD

    given, kv = call(
        pick_kernel, place, (og, prefix_keys, prefix_values), (bf(half, width), bf(RB, 2 * HD)), scratch=[pltpu.SemaphoreType.DMA((16,))],
        moved=2 << 20, aside=1,
    )
    w_sib = send(w_out, SIBLING)
    og_sib = send(given, SIBLING)

    kv_pair = jnp.concatenate([kv, send(kv, SIBLING)])
    kv_first = send(kv_pair, INWARD)
    p4, p3, p2, p1, p0, og_cat = call(
        upstream_kernel, place, (og, og_sib, w_out, w_sib),
        (bf(2 * RB, hq), bf(4 * RB, hq), bf(4 * RB, hq), bf(4 * RB, hq), bf(2 * RB, hq), bf(half, 2 * width)),
        scratch=[pltpu.SemaphoreType.DMA((17,))],
        flops=4 * half * hq * width, moved=6 << 20, aside=2,
    )
    ring1 = send(p4, OUTWARD)
    kv_second = send(kv_first, INWARD)
    step = jnp.concatenate([added(p3[:2 * RB], ring1), p3[2 * RB:]])
    ring2 = send(after(step, kv_first), OUTWARD)
    kv_third = send(kv_second, INWARD)
    ring3 = send(after(added(p2, ring2), kv_second), OUTWARD)
    kv_fourth = send(kv_third[:RB], INWARD)
    near_own = jnp.concatenate((kv, kv_first, kv_second, kv_third, kv_fourth))
    far_own = send(near_own, ACROSS)
    ring4 = send(after(added(p1, ring3), near_own), OUTWARD)
    near_sib = send(near_own, SIBLING)
    far_sib = send(after(far_own, ring3), SIBLING)
    keys = (near_own, far_own, near_sib, far_sib)
    ring_sib = send(ring4[2 * RB:], SIBLING)
    g_near = added(p0[:RB], ring4[:RB], ring_sib[:RB])
    g_give = added(p0[RB:], ring4[RB:2 * RB], ring_sib[RB:])
    g_far = send(g_give, ACROSS)

    o, log_total = call(
        forward_kernel, place, (q,) + keys, (bf(RB, hq), f32(1, HEADS * RB)),
        scratch=[pltpu.VMEM((rows, HEADS * RB), F32)],
        flops=4 * attention, moved=3 << 20, exps=HEADS * RB * rows,
    )
    dq, d_keep, d_give = call(
        backward_kernel, place, (q,) + keys + (g_near, g_far, o, log_total),
        (bf(RB, hq), bf(half, 2 * HD), bf(half, 2 * HD)),
        flops=10 * attention, moved=6 << 20, exps=HEADS * RB * rows,
    )

    dkv = added(d_keep, send(d_give, SIBLING))
    t4, t3, t2, t1, t0 = (dkv[a:b] for a, b in ((0, 256), (256, 768), (768, 1280), (1280, 1792), (1792, 2048)))
    o_pair = jnp.concatenate([o, send(after(o, dq), SIBLING)])
    o1 = send(o_pair, INWARD)
    turn1 = send(t4, OUTWARD)
    o2 = send(after(o1, turn1), INWARD)
    o_first = send(jnp.concatenate((o, o1, o2)), ACROSS)
    dq_pair = jnp.concatenate([dq, send(dq, ACROSS)])
    quad = jnp.concatenate([dq_pair, send(dq_pair, SIBLING)])
    turn2 = send(after(jnp.concatenate([added(t3[:2 * RB], turn1), t3[2 * RB:]]), dq_pair), OUTWARD)
    o3 = send(after(o2, turn2), INWARD)
    r1 = send(after(quad, turn1), INWARD)
    turn3 = send(after(added(t2, turn2), quad), OUTWARD)
    r2 = send(r1, INWARD)
    o4 = send(after(o3[:RB], turn3), INWARD)
    o_last = jnp.concatenate((o3, o4))
    turn4 = send(after(added(t1, turn3), r1), OUTWARD)
    r3 = send(r2, INWARD)
    s1 = send(r1, SIBLING)
    grad_hidden, total = call(
        hidden_kernel, place, (hidden[0], w_query, quad, r1, s1),
        (bf(rows, width), f32(width, hq)),
        flops=3 * rows * width * hq, moved=8 << 20,
    )
    turn_sib = send(after(turn4, r2, o_first, total)[2 * RB:], SIBLING)
    dkv_near = t0[:RB].astype(F32) + turn4[:RB].astype(F32) + turn_sib[:RB].astype(F32)
    dkv_far = send(added(t0[RB:], turn4[RB:2 * RB], turn_sib[RB:]), ACROSS)
    r4 = send(r3[:2 * RB], INWARD)
    o_second = send(after(o_last, dkv_far), ACROSS)
    dkv = (dkv_near + dkv_far.astype(F32)).astype(BF)
    s2, s3, s4 = (send(block, SIBLING) for block in (r2, r3, r4))
    dkv = after(dkv, r3)
    for pairs in (DP_X1, DP_X2, DP_Y):
        dkv = added(dkv, lax.ppermute(dkv, "dp", pairs))
    kv_low = dkv

    wo_own, wo_give = call(
        wo_kernel, place, (o, o1, o2, o_last, o_first, o_second, og_cat), (bf(hq, width), bf(hq, width)),
        flops=2 * half * hq * 2 * width, moved=5 << 20,
    )
    wo_got = send(wo_give, SIBLING)

    columns = prefix_hidden.shape[1]
    kv_cols = kv_low.T.reshape(2, 2, 2, 2, 2, 8, RB)
    for axis, bit in enumerate((y, z // 4, z // 2 % 2, z % 2, c)):
        kv_cols = jnp.where(bit == 1, jnp.flip(kv_cols, axis), kv_cols)
    kv_cols = jnp.transpose(kv_cols, (4, 1, 0, 2, 3, 5, 6)).reshape(2 * HD, RB)
    wkv = dot(after(kv_cols, r4), prefix_hidden, NN).astype(BF)
    grad_hidden, parts = call(
        last_kernel, place, (grad_hidden, hidden[0], w_query, r2, s2, r3, s3, r4, s4, total, wo_own, wo_got),
        (bf(rows, width), bf(1024, 256)),
        scratch=[
            pltpu.VMEM((20, RB, width), BF), pltpu.VMEM((20, RB, width), BF),
            pltpu.SemaphoreType.DMA((20,)), pltpu.SemaphoreType.DMA((20,)),
        ],
        flops=rows * width * hq, moved=3 << 20, aside=2, outs_aside=1, aliases={1: 0},
    )
    for pairs, earlier in ((SIBLING, r4), (Z4, r4), (ACROSS, parts), (Z2, parts), (Z1, parts)):
        size = wkv.shape[0] // 2
        got = send(after(wkv, earlier)[size:], pairs)
        wkv = added(wkv[:size], got) if size > 8 else wkv[:size].astype(F32) + got.astype(F32)
    grad_wkv = wkv
    parts = lax.all_to_all(parts.reshape(8, 128, 256), "dp", 0, 0)
    sums = jnp.sum(parts.astype(F32), axis=0)
    grad_wq = jnp.concatenate([sums[:32], sums[32:64]], axis=1)
    return grad_hidden[None], grad_wq, sums[64:], kv_low, grad_wkv


def solution(mesh):
    in_specs = (
        P("dp", "blk", None),
        P("blk", None),
        P("blk", None),
        P("dp", None, "blk"),
        P("dp", None, "blk"),
        P("blk", "dp"),
        P("blk", None),
        P(None, "blk"),
    )
    out_specs = (
        P("dp", None, "blk"),
        P(("blk", "dp"), None),
        P("dp", "blk"),
        P("blk", None),
        P("blk", "dp"),
    )
    return jax.shard_map(shards, mesh=mesh, in_specs=in_specs, out_specs=out_specs, check_vma=False)
```
